256 devices in a mesh: grp: 2 (over x_hi), wa: 128 (over z, x_lo, y, core).
Axes of the slice: x: 4 (x_hi: 2, x_lo: 2; x = x_hi * 2 + x_lo), y: 4, z: 8, core: 2. Of those that a mesh axis runs over, the one named last changes fastest.
Arguments:
- table: bfloat16 [1048576, 128], P(('grp', 'wa')), may hold values from -6 to 6
- owners: int32 [2, 16384, 8, 4], P('grp', 'wa'), may hold values from 0 to 127, all different within a row; in each aligned block of 1024 rows (0 to 1023, 1024 to 2047, ..., all dimensions but the last counted through in order) at most 64 rows name the same one
- local_rows: int32 [2, 16384, 8, 4], P('grp', 'wa'), may hold values from 0 to 4095
- lengths: int32 [2, 16384, 8], P('grp', 'wa'), may hold values from 2 to 4
- labels: float32 [16384], P('wa'), may hold values from 0 to 1
- w_first: bfloat16 [2048, 4096], P('grp'), may hold values from -0.125 to 0.125
- w_head: bfloat16 [4096], replicated, may hold values from -0.09375 to 0.09375
Outputs:
- logits: float32 [16384], P('wa')
- dense_grad: float32 [2048, 4096], P(('grp', 'wa'))
- head_grad: float32 [4096], P(('grp', 'wa'))
- row_grad: bfloat16 [1048576, 128], P(('grp', 'wa'))
The draws below stay inside these ranges and needn't reach their ends.
Inputs may be any that keep to these rules, and one draw needn't show every extreme that they name: Within the 1024 bags of one device's samples, each owner is named at most 64 times, a bound that some block reaches; the 4 owners of one bag differ.
All inputs are finite; a program needn't handle non-finite values.
Results may differ from the reference program's by a relative error of at most 0.007.
Values may be sent and summed in bfloat16 or wider, within the bound.
No kernel may reach another device: no remote copies, remote signals or barrier semaphores. Data moves between devices by JAX's collectives and lax.ppermute only.
A program may use at most 128 MiB of HBM per device.

```python
import math
import jax
import jax.numpy as jnp
import numpy as np
from jax import lax

E = 128
HID = 4096
L = 4
SMP_DEV = 128
ROWS_DEV = 4096
NBG = 8
FEAT = 2048
BATCH = 16384
TROWS = 1048576
CAP = 64
N_GRP = 2
N_WA = 128


def place_ends(entries, key, least, largest):
    spot = [jax.random.randint(jax.random.fold_in(key, axis), (), 0, length) for axis, length in enumerate(entries.shape)]
    main_axis = entries.shape.index(max(entries.shape))
    neighbour = spot[:main_axis] + [(spot[main_axis] + 1) % entries.shape[main_axis]] + spot[main_axis + 1:]
    return entries.at[tuple(spot)].set(least).at[tuple(neighbour)].set(largest)


def levels(stream_key, dims, shards, least, high):
    level = 1.0
    for dim, parts in shards:
        draws = jax.random.uniform(jax.random.fold_in(jax.random.fold_in(stream_key, 6), dim), (parts,), jnp.float32, least / len(shards), high / len(shards))
        level = level * jnp.repeat(jnp.exp(draws), dims[dim] // parts).reshape((-1,) + (1,) * (len(dims) - 1 - dim))
    return level


def rank_bounds(amount, lean):
    weights = [(1 << 20) // math.isqrt(rank ** lean) + 1 for rank in range(1, amount + 1)]
    width = 1 + sum(weights) // (1 << 30)
    return np.cumsum(np.array([max(1, weight // width) for weight in weights]))


def ranked(own_key, shape, amount, lean):
    listing = rank_bounds(amount, lean)
    lot = jax.random.randint(jax.random.fold_in(own_key, 1), shape, 0, int(listing[amount - 1]))
    rank = jnp.searchsorted(jnp.asarray(listing, jnp.int32), lot, side="right")
    return jax.random.permutation(jax.random.fold_in(own_key, 2), amount)[rank].astype(jnp.int32)


def routed_block(stream_key, own, number, rows, count, top, reach, lean):
    order = jax.random.permutation(stream_key, count)
    crowded, ordinary = portions_of(count, rows * top, reach, lean, True), portions_of(count, rows * top, reach, lean, False)
    places = jnp.arange(count)

    def named(sizes, rotation):
        used = int((sizes > 0).sum())
        fixed = max(1, used // 4)
        shifted = fixed + (places - fixed + rotation * (used - fixed)) % max(1, count - fixed)
        return jnp.zeros((count,), jnp.int32).at[order[jnp.where(places < fixed, places, shifted)]].set(jnp.asarray(sizes, jnp.int32))

    sizes = jnp.where(number % 4 == 0, named(crowded, number // 4), named(ordinary, number - number // 4 - 1))
    mixed = jax.random.permutation(jax.random.fold_in(own, 3), count)
    donor, receiver = mixed[0:count // 2 * 2:2], mixed[1:count // 2 * 2:2]
    slack = jnp.minimum(sizes[donor] - 1, reach - sizes[receiver]) // 2
    slack = jnp.where((donor == order[0]) | (receiver == order[0]) | (sizes[receiver] == 0), 0, jnp.maximum(slack, 0))
    shifted = jax.random.randint(jax.random.fold_in(own, 4), (count // 2,), 0, 1 << 20) % (slack + 1)
    sizes = sizes.at[donor].add(-shifted).at[receiver].add(shifted)
    members = jnp.searchsorted(jnp.cumsum(sizes), jnp.arange(rows * top), side="right").astype(jnp.int32)
    listing = members.reshape(top, rows).T
    listing = listing[jax.random.permutation(jax.random.fold_in(own, 1), rows)]
    rotation = jax.random.randint(jax.random.fold_in(own, 2), (rows, 1), 0, top)
    return jnp.take_along_axis(listing, (jnp.arange(top)[None, :] + rotation) % top, axis=1)


def portions_of(number_of, total, most, lean, full):
    weights = [(1 << 20) // math.isqrt(grade ** lean) + 1 for grade in range(1, number_of + 1)]
    largest = most if full else min(most, max(-(-total // number_of), total * weights[0] // sum(weights)))
    least = 1 if total - largest >= number_of - 1 else 0
    holding, surplus = [largest] + [least] * (number_of - 1), total - largest - least * (number_of - 1)
    while surplus > 0:
        free = [i for i in range(1, number_of) if holding[i] < largest] or [i for i in range(1, number_of) if holding[i] < most]
        pool, left = sum([weights[i] for i in free]), surplus
        for i in free:
            addition = min(most - holding[i], max(1, left * weights[i] // pool), surplus)
            holding[i] = holding[i] + addition
            surplus = surplus - addition
    return np.array(holding)


def centred(key, extent, width, limit, split=(), kind=jnp.bfloat16):
    values = width * jax.random.normal(key, extent, jnp.float32)
    if split:
        values = values * levels(key, extent, split, -0.22, 0.18)
    return jnp.clip(values, -limit, limit).astype(kind)


def setup_inputs(seed: int = 0) -> dict:
    splits = jax.random.split(jax.random.key(seed), 8)
    table = centred(splits[0], (TROWS, E), 1.0, 6.0, ((0, 256),))
    owners_keys = jax.random.split(jax.random.fold_in(splits[1], 1), N_GRP * BATCH * NBG // (SMP_DEV * NBG))
    owners_turns = jax.random.permutation(jax.random.fold_in(splits[1], 3), N_GRP * BATCH * NBG // (SMP_DEV * NBG))
    owners = jax.vmap(lambda own, number: routed_block(jax.random.fold_in(splits[1], 2), own, number, SMP_DEV * NBG, N_WA, L, CAP, 2))(owners_keys, owners_turns).reshape((N_GRP, BATCH, NBG, L))
    local_rows = place_ends(ranked(splits[2], (N_GRP, BATCH, NBG, L), ROWS_DEV, 2), jax.random.fold_in(splits[2], 3), 0, ROWS_DEV - 1).astype(jnp.int32)
    lengths = place_ends(jax.random.randint(splits[3], (N_GRP, BATCH, NBG), 2, L + 1), jax.random.fold_in(splits[3], 1), 2, L).astype(jnp.int32)
    labels = jnp.clip(1.0 * jax.random.uniform(splits[4], (BATCH,), jnp.float32) ** levels(splits[4], (BATCH,), ((0, 128),), -0.2, 0.2), 0.0, 1.0)
    w_first = centred(splits[5], (FEAT, HID), FEAT ** -0.5, 0.125, ((0, 2),))
    w_head = centred(splits[6], (HID,), HID ** -0.5, 0.09375)
    return dict(table=table, owners=owners, local_rows=local_rows, lengths=lengths, labels=labels, w_first=w_first, w_head=w_head)


def reference(table, owners, local_rows, lengths, labels, w_first, w_head):
    group_ids = jnp.arange(N_GRP, dtype=jnp.int32)[:, None, None, None]
    rows = (group_ids * N_WA + owners) * ROWS_DEV + local_rows
    live = jnp.arange(L, dtype=jnp.int32)[None, None, None, :] < lengths[..., None]

    def add_slot(total, index):
        slot_rows = lax.dynamic_index_in_dim(rows, index, 3, False)
        keep = lax.dynamic_index_in_dim(live, index, 3, False)
        tiles = table[slot_rows].astype(jnp.float32)
        return total + jnp.where(keep[..., None], tiles, jnp.float32(0.0)), None

    pooled, _ = lax.scan(add_slot, jnp.zeros((N_GRP, BATCH, NBG, E), jnp.float32), jnp.arange(L, dtype=jnp.int32))
    pooled = pooled.astype(jnp.bfloat16)
    features = jnp.transpose(pooled, (1, 0, 2, 3)).reshape(BATCH, FEAT)
    pre = jnp.dot(features, w_first, preferred_element_type=jnp.float32)
    hidden = jax.nn.silu(pre).astype(jnp.bfloat16)
    logits = jnp.dot(hidden, w_head, preferred_element_type=jnp.float32)
    dlogit = jax.nn.sigmoid(logits) - labels
    gate = jax.nn.sigmoid(pre)
    slope = gate * (1.0 + pre * (1.0 - gate))
    grad_hidden = (dlogit[:, None] * w_head.astype(jnp.float32)[None, :] * slope).astype(jnp.bfloat16)
    dense_grad = lax.dot_general(features, grad_hidden, (((0,), (0,)), ((), ())), preferred_element_type=jnp.float32)
    head_grad = jnp.dot(dlogit, hidden.astype(jnp.float32), precision=lax.Precision.HIGHEST)
    pooled_grad = lax.dot_general(grad_hidden, w_first, (((1,), (1,)), ((), ())), preferred_element_type=jnp.float32)
    pooled_grad = pooled_grad.astype(jnp.bfloat16).astype(jnp.float32)
    pooled_grad = jnp.transpose(pooled_grad.reshape(BATCH, N_GRP, NBG, E), (1, 0, 2, 3))

    def add_grads(total, index):
        slot_rows = lax.dynamic_index_in_dim(rows, index, 3, False)
        keep = lax.dynamic_index_in_dim(live, index, 3, False)
        terms = jnp.where(keep[..., None], pooled_grad, jnp.float32(0.0))
        return total.at[slot_rows.reshape(-1)].add(terms.reshape(-1, E)), None

    row_grad, _ = lax.scan(add_grads, jnp.zeros((TROWS, E), jnp.float32), jnp.arange(L, dtype=jnp.int32))
    return logits, dense_grad, head_grad, row_grad.astype(jnp.bfloat16)
```

```python
import functools

import jax
import jax.numpy as jnp
from jax import lax
from jax.experimental import pallas as pl
from jax.experimental.pallas import tpu as pltpu
from jax.sharding import PartitionSpec as P

BF16 = jnp.bfloat16
F32 = jnp.float32
I32 = jnp.int32
E = 128
CAP = 64
ROWS_BITS = 12
LIMIT = pltpu.CompilerParams(vmem_limit_bytes=56 * 1024 * 1024)
NT = (((1,), (1,)), ((), ()))


def one_hot(left, right):
    return jnp.where(left == right, 1.0, 0.0).astype(BF16)


def route_kernel(code_ref, ids_ref, bag_ref, bag_t_ref):
    lines = code_ref.shape[0]
    owners = ids_ref.shape[0]
    pairs = owners // 2
    sub = lax.broadcasted_iota(I32, (owners, E), 0)
    half_sub = lax.broadcasted_iota(I32, (CAP, E), 0)
    pair_sub = lax.broadcasted_iota(I32, (pairs, E), 0)
    lane = lax.broadcasted_iota(I32, (1, E), 1)
    before = one_hot(
        jnp.where(lax.broadcasted_iota(I32, (E, E), 0) < lax.broadcasted_iota(I32, (E, E), 1), 1, 0), 1
    )
    features = lines // 4
    carry = jnp.zeros((owners, 1), F32)
    ids_hi = jnp.zeros((owners, CAP), F32)
    ids_lo = jnp.zeros((owners, CAP), F32)
    bag = jnp.zeros((pairs, 2 * E), F32)
    bag_t = jnp.zeros((2 * E, pairs), F32)
    for k in range(lines):
        code = code_ref[k : k + 1, :]
        owner = code >> ROWS_BITS
        local = code & ((1 << ROWS_BITS) - 1)
        number = (k % features) * E + lane + 1
        named = jnp.where(sub == owner, 1.0, 0.0)
        named_b = named.astype(BF16)
        rank = jnp.dot(named_b, before, preferred_element_type=F32) + carry
        carry = carry + jnp.sum(named, axis=1, keepdims=True)
        position = jnp.sum(named * rank, axis=0, keepdims=True).astype(I32)
        place = jnp.where(half_sub == position, 1.0, 0.0)
        place_hi = (place * (local >> 6).astype(F32)).astype(BF16)
        place_lo = (place * (local & 63).astype(F32)).astype(BF16)
        ids_hi += lax.dot_general(named_b, place_hi, NT, preferred_element_type=F32)
        ids_lo += lax.dot_general(named_b, place_lo, NT, preferred_element_type=F32)
        spot = jnp.where(sub == (owner & 1) * CAP + position, 1.0, 0.0)
        spot2 = jnp.concatenate(
            [(spot * (number >> 5).astype(F32)).astype(BF16), (spot * (number & 31).astype(F32)).astype(BF16)], axis=0
        )
        in_pair = one_hot(pair_sub, owner >> 1)
        bag += lax.dot_general(in_pair, spot2, NT, preferred_element_type=F32)
        bag_t += lax.dot_general(spot2, in_pair, NT, preferred_element_type=F32)
    ids_ref[...] = (ids_hi * 64.0 + ids_lo).astype(I32)
    bag_ref[...] = (bag[:, :E] * 32.0 + bag[:, E:]).astype(I32) - 1
    bag_t_ref[...] = (bag_t[:E, :] * 32.0 + bag_t[E:, :]).astype(I32) - 1


def gather_kernel(ids_ref, table_ref, out_ref, spread):
    sources = ids_ref.shape[0]
    ids_t = jnp.transpose(ids_ref[...].astype(F32)).astype(I32)
    for s in range(sources):
        spread[s * CAP : (s + 1) * CAP, :] = jnp.broadcast_to(ids_t[:, s : s + 1], (CAP, E))
    rows = table_ref.shape[0]
    block = 1024
    depth = 1024
    lane = lax.broadcasted_iota(I32, (1, E), 1)

    def body(i, _):
        wanted = spread[pl.ds(pl.multiple_of(i * block, block), block), :]
        total = jnp.zeros((block, E), F32)
        for d in range(rows // depth):
            parts = [one_hot(wanted, lane + (d * depth + m * E)) for m in range(depth // E)]
            total += jnp.dot(
                jnp.concatenate(parts, axis=1),
                table_ref[d * depth : (d + 1) * depth, :],
                preferred_element_type=F32,
            )
        out_ref[pl.ds(pl.multiple_of(i * block, block), block), :] = total.astype(BF16)
        return 0

    lax.fori_loop(0, sources * CAP // block, body, 0)


def sum_rows(lists_ref, data_ref, base, count):
    chunk = 8
    sub = lax.broadcasted_iota(I32, (count, E), 0) + base

    def body(i, total):
        lists = lists_ref[pl.ds(pl.multiple_of(i * chunk, chunk), chunk), :]
        parts = [one_hot(sub, lists[m : m + 1, :]) for m in range(chunk)]
        return total + jnp.dot(
            jnp.concatenate(parts, axis=1),
            data_ref[pl.ds(pl.multiple_of(i * chunk * E, chunk * E), chunk * E), :],
            preferred_element_type=F32,
        )

    return lax.fori_loop(0, lists_ref.shape[0] // chunk, body, jnp.zeros((count, E), F32))


def pool_kernel(bag_ref, rows_ref, w_ref, pooled_ref, part_ref):
    bags = pooled_ref.shape[1] // E * pooled_ref.shape[0]
    samples = pooled_ref.shape[0]
    pooled = sum_rows(bag_ref, rows_ref, 0, bags).astype(BF16)
    for f in range(bags // samples):
        pooled_ref[:, f * E : (f + 1) * E] = pooled[f * samples : (f + 1) * samples, :]
    step = 512
    for j in range(w_ref.shape[1] // step):
        part_ref[:, j * step : (j + 1) * step] = jnp.dot(
            pooled_ref[...], w_ref[:, j * step : (j + 1) * step], preferred_element_type=F32
        ).astype(BF16)


def head_kernel(mine_ref, other_ref, labels_ref, w_head_ref, logits_ref, grad_ref, head_ref):
    pieces, samples, width = grad_ref.shape
    logits = jnp.zeros((samples, 1), F32)
    for q in range(pieces):
        cols = slice(q * width, (q + 1) * width)
        pre = mine_ref[:, cols].astype(F32) + other_ref[:, cols].astype(F32)
        hidden = (pre * jax.nn.sigmoid(pre)).astype(BF16).astype(F32)
        logits += jnp.sum(hidden * w_head_ref[:, cols].astype(F32), axis=1, keepdims=True)
    logits_ref[...] = logits
    dlogit = jax.nn.sigmoid(logits) - labels_ref[...]
    for q in range(pieces):
        cols = slice(q * width, (q + 1) * width)
        pre = mine_ref[:, cols].astype(F32) + other_ref[:, cols].astype(F32)
        gate = jax.nn.sigmoid(pre)
        hidden = (pre * gate).astype(BF16).astype(F32)
        head_ref[:, cols] = jnp.sum(hidden * dlogit, axis=0, keepdims=True)
        slope = gate * (1.0 + pre * (1.0 - gate))
        grad_ref[q] = (dlogit * w_head_ref[:, cols].astype(F32) * slope).astype(BF16)


def back_kernel(grad_ref, w_ref, bag_t_ref, out_ref, pooled_grad):
    pieces, samples, width = grad_ref.shape
    bags = pooled_grad.shape[0]
    half = w_ref.shape[0] // 2
    for h in range(2):
        total = jnp.zeros((samples, half), F32)
        for q in range(pieces):
            total += lax.dot_general(
                grad_ref[q],
                w_ref[h * half : (h + 1) * half, q * width : (q + 1) * width],
                NT,
                preferred_element_type=F32,
            )
        for f in range(half // E):
            b = h * (half // E) + f
            pooled_grad[b * samples : (b + 1) * samples, :] = total[:, f * E : (f + 1) * E].astype(BF16)
    lane = lax.broadcasted_iota(I32, (1, E), 1)
    together = 8
    for k in range(0, bag_t_ref.shape[1], together):
        wanted = jnp.concatenate(
            [jnp.broadcast_to(bag_t_ref[:, k + m : k + m + 1], (E, E)) for m in range(together)], axis=0
        )
        parts = [one_hot(wanted, lane + b * E) for b in range(bags // E)]
        out_ref[k * E : (k + together) * E, :] = jnp.dot(
            jnp.concatenate(parts, axis=1), pooled_grad[...], preferred_element_type=F32
        ).astype(BF16)


def dense_kernel(*refs):
    out_ref = refs[-1]
    count = (len(refs) - 1) // 2
    features = [r for r in refs[:count]]
    grads = [r for r in refs[count : 2 * count]]
    left = jnp.concatenate([r[...].reshape(-1, r.shape[-1]) for r in features], axis=0)
    right = jnp.concatenate([r[...].reshape(-1, r.shape[-1]) for r in grads], axis=0)
    out_ref[...] = lax.dot_general(
        left, right, (((0,), (0,)), ((), ())), preferred_element_type=F32
    ).astype(out_ref.dtype)


def scatter_kernel(ids_ref, data_ref, out_ref):
    rows = out_ref.shape[0]
    block = 1024

    def body(i, _):
        start = pl.multiple_of(i * block, block)
        out_ref[pl.ds(start, block), :] = sum_rows(ids_ref, data_ref, i * block, block).astype(BF16)
        return 0

    lax.fori_loop(0, rows // block, body, 0)


def call(kernel, outs, flops, moved, scratch=()):
    return pl.pallas_call(
        kernel,
        out_shape=outs,
        scratch_shapes=list(scratch),
        compiler_params=LIMIT,
        cost_estimate=pl.CostEstimate(flops=flops, bytes_accessed=moved, transcendentals=0),
    )


def shape(dims, kind):
    return jax.ShapeDtypeStruct(dims, kind)


def shards(table, owners, local_rows, lengths, labels, w_first, w_head):
    count = lax.axis_size("wa")
    samples = labels.shape[0]
    bags_here = owners.shape[2]
    depth = owners.shape[3]
    hidden_width = w_head.shape[0]
    feats = bags_here * E
    slots = count * CAP
    place = lax.axis_index("wa")
    group = lax.axis_index("grp")
    y = (place // 2) % 4
    core = place % 2
    x_low = (place // 8) % 2

    def spot(z, x, yy, c):
        return ((z * 2 + x) * 4 + yy % 4) * 2 + c

    def where_of(w):
        return w // 16, (w // 8) % 2, (w // 2) % 4, w % 2

    def moved(step):
        return [(w, spot(*step(*where_of(w)))) for w in range(count)]

    to_mate = moved(lambda z, x, yy, c: (z, x, yy, 1 - c))
    to_x = moved(lambda z, x, yy, c: (z, 1 - x, yy, c))
    to_y = [moved(lambda z, x, yy, c, d=d: (z, x, yy + d, c)) for d in (1, 3, 2)]
    z_groups = [[z * 16 + r for z in range(8)] for r in range(16)]
    yc_groups = [[g * 8 + r for r in range(8)] for g in range(16)]

    live = jnp.arange(depth, dtype=I32) < lengths[0][:, :, None]
    code = jnp.where(live, owners[0] * (1 << ROWS_BITS) + local_rows[0], -1)
    code = jnp.transpose(code, (2, 1, 0)).reshape(depth * bags_here, samples)
    ids, bag, bag_t = call(
        route_kernel,
        (shape((count, CAP), I32), shape((count // 2, 2 * CAP), I32), shape((2 * CAP, count // 2), I32)),
        2 * 4096 * 128 * 1024,
        100000,
    )(code)
    ids_in = lax.all_to_all(ids, "wa", split_axis=0, concat_axis=0, tiled=True)
    tiles = call(
        gather_kernel,
        shape((slots, E), BF16),
        2 * slots * 4096 * E,
        4 << 20,
        [pltpu.VMEM((slots, E), I32)],
    )(ids_in, table)
    returned = lax.all_to_all(
        tiles.reshape(count, CAP, E), "wa", split_axis=0, concat_axis=0, tiled=True
    ).reshape(slots, E)
    pooled, part = call(
        pool_kernel,
        (shape((samples, feats), BF16), shape((samples, hidden_width), BF16)),
        2 * slots * 1024 * E + 2 * samples * feats * hidden_width,
        12 << 20,
    )(bag, returned, w_first)
    other = lax.ppermute(part, "grp", [(0, 1), (1, 0)])

    mate_pooled = lax.ppermute(pooled, "wa", to_mate)
    both_pooled = jnp.concatenate([pooled, mate_pooled], axis=0)
    all_pooled = [both_pooled] + [lax.ppermute(both_pooled, "wa", p) for p in to_y]

    logits, grad, head = call(
        head_kernel,
        (
            shape((samples, 1), F32),
            shape((8, samples, hidden_width // 8), BF16),
            shape((1, hidden_width), F32),
        ),
        samples * hidden_width * 60,
        4 << 20,
    )(part, other, labels.reshape(samples, 1), w_head.reshape(1, hidden_width))

    width = hidden_width // 8
    grad4 = grad.reshape(4, 2, samples, width)
    keep = lax.dynamic_index_in_dim(grad4, core, 1, False)
    mate_grad = lax.ppermute(lax.dynamic_index_in_dim(grad4, 1 - core, 1, False), "wa", to_mate)
    pairs = jnp.concatenate([keep, mate_grad], axis=1)

    def piece(d):
        return lax.dynamic_index_in_dim(pairs, (y + d) % 4, 0, False)

    all_grad = [piece(0)] + [lax.ppermute(piece(d), "wa", p) for d, p in zip((1, 3, 2), to_y)]

    send = call(
        back_kernel,
        shape((slots, E), BF16),
        2 * slots * 1024 * E + 2 * samples * feats * hidden_width,
        12 << 20,
        [pltpu.VMEM((samples * bags_here, E), BF16)],
    )(grad, w_first, bag_t)
    arrived = lax.all_to_all(
        send.reshape(count, CAP, E), "wa", split_axis=0, concat_axis=0, tiled=True
    ).reshape(slots, E)

    dense = call(
        dense_kernel, shape((feats, width), BF16), 2 * feats * width * 8 * samples, 4 << 20
    )(*all_pooled, *all_grad)
    dense = dense.reshape(8, 2, feats // 16, width)
    mine = lax.dynamic_index_in_dim(dense, x_low, 1, False)
    theirs = lax.ppermute(lax.dynamic_index_in_dim(dense, 1 - x_low, 1, False), "wa", to_x)
    partial = (mine.astype(F32) + theirs.astype(F32)).astype(BF16)
    by_z = lax.all_to_all(partial, "wa", 0, 0, axis_index_groups=z_groups, tiled=True)
    block = jnp.sum(by_z.astype(F32), axis=0).reshape(8, 8, width)
    turned = lax.all_to_all(block, "wa", 0, 0, axis_index_groups=yc_groups, tiled=True)
    dense_grad = jnp.transpose(turned, (1, 0, 2)).reshape(8, hidden_width)

    head_share = lax.dynamic_slice_in_dim(head[0], group * (hidden_width // 2), hidden_width // 2)
    head_in = lax.all_to_all(
        head_share.reshape(count, hidden_width // 2 // count), "wa", split_axis=0, concat_axis=0, tiled=True
    )
    head_grad = jnp.sum(head_in, axis=0)

    row_grad = call(
        scatter_kernel, shape((table.shape[0], E), BF16), 2 * slots * 4096 * E, 4 << 20
    )(ids_in.reshape(count // 2, 2 * CAP), arrived)
    return (logits.reshape(samples), dense_grad, head_grad, row_grad)


def solution(mesh):
    return jax.shard_map(
        shards,
        mesh=mesh,
        in_specs=(
            P(("grp", "wa"), None),
            P("grp", "wa", None, None),
            P("grp", "wa", None, None),
            P("grp", "wa", None),
            P("wa"),
            P("grp", None),
            P(),
        ),
        out_specs=(P("wa"), P(("grp", "wa"), None), P(("grp", "wa")), P(("grp", "wa"), None)),
        check_vma=False,
    )
```

```python
import functools

import jax
import jax.numpy as jnp
from jax import lax
from jax.experimental import pallas as pl
from jax.experimental.pallas import tpu as pltpu
from jax.sharding import PartitionSpec as P

BF16 = jnp.bfloat16
F32 = jnp.float32
I32 = jnp.int32
E = 128
CAP = 64
ROWS_BITS = 12
LOW_BITS = 8
LOW = 1 << LOW_BITS
LIMIT = pltpu.CompilerParams(vmem_limit_bytes=56 * 1024 * 1024)
NT = (((1,), (1,)), ((), ()))


def one_hot(left, right):
    return jnp.where(left == right, 1.0, 0.0).astype(BF16)


def route_kernel(code_ref, ids_ref, bag_ref, bag_t_ref):
    lines = code_ref.shape[0]
    owners = ids_ref.shape[0]
    pairs = owners // 2
    sub = lax.broadcasted_iota(I32, (owners, E), 0)
    half_sub = lax.broadcasted_iota(I32, (CAP, E), 0)
    pair_sub = lax.broadcasted_iota(I32, (pairs, E), 0)
    lane = lax.broadcasted_iota(I32, (1, E), 1)
    before = one_hot(
        jnp.where(lax.broadcasted_iota(I32, (E, E), 0) < lax.broadcasted_iota(I32, (E, E), 1), 1, 0), 1
    )
    features = lines // 4
    carry = jnp.zeros((owners, 1), F32)
    ids_hi = jnp.zeros((owners, CAP), F32)
    ids_lo = jnp.zeros((owners, CAP), F32)
    bag = jnp.zeros((pairs, 2 * E), F32)
    bag_t = jnp.zeros((2 * E, pairs), F32)
    for k in range(lines):
        code = code_ref[k : k + 1, :]
        owner = code >> ROWS_BITS
        local = code & ((1 << ROWS_BITS) - 1)
        number = (k % features) * E + lane + 1
        named = jnp.where(sub == owner, 1.0, 0.0)
        named_b = named.astype(BF16)
        rank = jnp.dot(named_b, before, preferred_element_type=F32) + carry
        carry = carry + jnp.sum(named, axis=1, keepdims=True)
        position = jnp.sum(named * rank, axis=0, keepdims=True).astype(I32)
        place = jnp.where(half_sub == position, 1.0, 0.0)
        place_hi = (place * (local >> 6).astype(F32)).astype(BF16)
        place_lo = (place * (local & 63).astype(F32)).astype(BF16)
        ids_hi += lax.dot_general(named_b, place_hi, NT, preferred_element_type=F32)
        ids_lo += lax.dot_general(named_b, place_lo, NT, preferred_element_type=F32)
        spot = jnp.where(sub == (owner & 1) * CAP + position, 1.0, 0.0)
        spot2 = jnp.concatenate(
            [(spot * (number >> 5).astype(F32)).astype(BF16), (spot * (number & 31).astype(F32)).astype(BF16)], axis=0
        )
        in_pair = one_hot(pair_sub, owner >> 1)
        bag += lax.dot_general(in_pair, spot2, NT, preferred_element_type=F32)
        bag_t += lax.dot_general(spot2, in_pair, NT, preferred_element_type=F32)
    ids_ref[...] = (ids_hi * 64.0 + ids_lo).astype(I32)
    bag_ref[...] = (bag[:, :E] * 32.0 + bag[:, E:]).astype(I32) - 1
    bag_t_ref[...] = (bag_t[:E, :] * 32.0 + bag_t[E:, :]).astype(I32) - 1


def spread_columns(lists_t, rows, out_ref):
    for c in range(lists_t.shape[1]):
        out_ref[c * rows : (c + 1) * rows, :] = jnp.broadcast_to(lists_t[:, c : c + 1], (rows, E))


def by_high(data, wide_ref):
    for h in range(data.shape[0] // LOW):
        wide_ref[:, h * E : (h + 1) * E] = data[h * LOW : (h + 1) * LOW, :]


def pick_rows(wanted_ref, wide_ref, out_ref, block):
    lane = lax.broadcasted_iota(I32, (1, E), 1)

    def body(i, _):
        start = pl.multiple_of(i * block, block)
        wanted = wanted_ref[pl.ds(start, block), :]
        low = wanted & (LOW - 1)
        high = wanted >> LOW_BITS
        left = jnp.concatenate([one_hot(low, lane + m * E) for m in range(LOW // E)], axis=1)
        total = jnp.zeros((block, E), F32)
        for h in range(0, wide_ref.shape[1] // E, 2):
            both = jnp.dot(left, wide_ref[:, h * E : (h + 2) * E], preferred_element_type=F32)
            total = jnp.where(high == h, both[:, :E], total)
            total = jnp.where(high == h + 1, both[:, E:], total)
        out_ref[pl.ds(start, block), :] = total.astype(BF16)
        return 0

    lax.fori_loop(0, out_ref.shape[0] // block, body, 0)


def sum_rows(lists_ref, high_ref, data_ref, total_ref):
    chunk = 8
    size = chunk * E
    sub = lax.broadcasted_iota(I32, (LOW, E), 0)
    total_ref[...] = jnp.zeros_like(total_ref)

    def body(i, _):
        start = pl.multiple_of(i * size, size)
        lists = lists_ref[pl.ds(pl.multiple_of(i * chunk, chunk), chunk), :] & (LOW - 1)
        left = jnp.concatenate([one_hot(sub, lists[m : m + 1, :]) for m in range(chunk)], axis=1)
        high = high_ref[pl.ds(start, size), :]
        data = data_ref[pl.ds(start, size), :]
        for h in range(0, total_ref.shape[1] // E, 2):
            right = jnp.concatenate(
                [jnp.where(high == jnp.array(g, BF16), data, jnp.array(0, BF16)) for g in (h, h + 1)], axis=1
            )
            total_ref[:, h * E : (h + 2) * E] += jnp.dot(left, right, preferred_element_type=F32)
        return 0

    lax.fori_loop(0, lists_ref.shape[0] // chunk, body, 0)


def gather_kernel(ids_ref, table_ref, out_ref, spread, wide):
    ids_t = jnp.transpose(ids_ref[...].astype(F32)).astype(I32)
    spread_columns(ids_t, CAP, spread)
    by_high(table_ref, wide)
    pick_rows(spread, wide, out_ref, 1024)


def pool_kernel(bag_ref, bag_t_ref, rows_ref, w_ref, pooled_ref, part_ref, high, total):
    samples = pooled_ref.shape[0]
    spread_columns((bag_t_ref[...] >> LOW_BITS).astype(F32).astype(BF16), E, high)
    sum_rows(bag_ref, high, rows_ref, total)
    for f in range(pooled_ref.shape[1] // E):
        h, low = divmod(f * samples, LOW)
        pooled_ref[:, f * E : (f + 1) * E] = total[low : low + samples, h * E : (h + 1) * E].astype(BF16)
    step = 512
    for j in range(w_ref.shape[1] // step):
        part_ref[:, j * step : (j + 1) * step] = jnp.dot(
            pooled_ref[...], w_ref[:, j * step : (j + 1) * step], preferred_element_type=F32
        ).astype(BF16)


def peer(where_ref, e, sign):
    return (where_ref[1] + sign * (e // 2) + 4) % 4 * 2 + (where_ref[2] + e % 2) % 2


def head_kernel(where_ref, mine_ref, other_ref, labels_ref, w_head_ref, logits_ref, head_ref, grad_ref, *piece_refs):
    pieces, samples, width = grad_ref.shape
    logits = jnp.zeros((samples, 1), F32)
    for q in range(pieces):
        cols = slice(q * width, (q + 1) * width)
        pre = mine_ref[:, cols].astype(F32) + other_ref[:, cols].astype(F32)
        hidden = (pre * jax.nn.sigmoid(pre)).astype(BF16).astype(F32)
        logits += jnp.sum(hidden * w_head_ref[:, cols].astype(F32), axis=1, keepdims=True)
    logits_ref[...] = logits
    dlogit = jax.nn.sigmoid(logits) - labels_ref[...]
    for q in range(pieces):
        cols = slice(q * width, (q + 1) * width)
        pre = mine_ref[:, cols].astype(F32) + other_ref[:, cols].astype(F32)
        gate = jax.nn.sigmoid(pre)
        hidden = (pre * gate).astype(BF16).astype(F32)
        head_ref[:, cols] = jnp.sum(hidden * dlogit, axis=0, keepdims=True)
        slope = gate * (1.0 + pre * (1.0 - gate))
        grad_ref[q] = (dlogit * w_head_ref[:, cols].astype(F32) * slope).astype(BF16)
    for e in range(pieces):
        piece_refs[e][...] = grad_ref[peer(where_ref, e, 1)]


def back_kernel(grad_ref, w_ref, bag_t_ref, out_ref, spread, wide):
    pieces, samples, width = grad_ref.shape
    half = w_ref.shape[0] // 2
    spread_columns(bag_t_ref[...], E, spread)
    for h in range(2):
        total = jnp.zeros((samples, half), F32)
        for q in range(pieces):
            total += lax.dot_general(
                grad_ref[q],
                w_ref[h * half : (h + 1) * half, q * width : (q + 1) * width],
                NT,
                preferred_element_type=F32,
            )
        for f in range(half // E):
            high, low = divmod((h * (half // E) + f) * samples, LOW)
            wide[low : low + samples, high * E : (high + 1) * E] = total[:, f * E : (f + 1) * E].astype(BF16)
    pick_rows(spread, wide, out_ref, 1024)


def dense_kernel(where_ref, features_ref, *refs):
    grad_refs, (mine_ref, send_ref, left) = refs[:8], refs[8:]
    samples = grad_refs[0].shape[0]
    for e in range(8):
        left[e * samples : (e + 1) * samples, :] = features_ref[
            pl.ds(pl.multiple_of(peer(where_ref, e, -1) * samples, samples), samples), :
        ]
    right = jnp.concatenate([r[...] for r in grad_refs], axis=0)
    half = mine_ref.shape[1]
    for z in range(mine_ref.shape[0]):
        both = lax.dot_general(
            left[:, 2 * half * z : 2 * half * (z + 1)], right, (((0,), (0,)), ((), ())), preferred_element_type=F32
        )
        own = where_ref[3] == 0
        mine_ref[z] = jnp.where(own, both[:half], both[half:])
        send_ref[z] = jnp.where(own, both[half:], both[:half]).astype(BF16)


def cross_kernel(where_ref, mine_ref, theirs_ref, keep_ref, *piece_refs):
    for d in range(8):
        z = (where_ref[0] + d) % 8
        block = mine_ref[z] + theirs_ref[z].astype(F32)
        if d == 0:
            keep_ref[...] = block
        else:
            piece_refs[d - 1][...] = block.astype(BF16)


def fold_kernel(where_ref, keep_ref, *refs):
    total = refs[-1]
    total[...] = keep_ref[...]
    for r in refs[:7]:
        total[...] += r[...].astype(F32)
    for e in range(8):
        refs[7 + e][...] = total[pl.ds(pl.multiple_of(peer(where_ref, e, 1) * 8, 8), 8), :]


def join_kernel(where_ref, *refs):
    out_ref = refs[-1]
    for e in range(8):
        width = refs[e].shape[1]
        start = pl.multiple_of(peer(where_ref, e, -1) * width, width)
        out_ref[:, pl.ds(start, width)] = refs[e][...]


def scatter_kernel(ids_ref, ids2_ref, data_ref, out_ref, high, total):
    ids_t = jnp.transpose((ids_ref[...] >> LOW_BITS).astype(F32)).astype(BF16)
    spread_columns(ids_t, CAP, high)
    sum_rows(ids2_ref, high, data_ref, total)
    for h in range(out_ref.shape[0] // LOW):
        out_ref[h * LOW : (h + 1) * LOW, :] = total[:, h * E : (h + 1) * E].astype(BF16)


def call(kernel, outs, flops, moved, scratch=(), placed=None):
    specs = {}
    if placed is not None:
        specs["in_specs"] = [pl.BlockSpec(memory_space=pltpu.SMEM)] + [pl.BlockSpec(memory_space=pltpu.VMEM)] * placed
    return pl.pallas_call(
        kernel,
        out_shape=outs,
        **specs,
        scratch_shapes=list(scratch),
        compiler_params=LIMIT,
        cost_estimate=pl.CostEstimate(flops=flops, bytes_accessed=moved, transcendentals=0),
    )


def shape(dims, kind):
    return jax.ShapeDtypeStruct(dims, kind)


def shards(table, owners, local_rows, lengths, labels, w_first, w_head):
    count = lax.axis_size("wa")
    samples = labels.shape[0]
    bags_here = owners.shape[2]
    depth = owners.shape[3]
    hidden_width = w_head.shape[0]
    feats = bags_here * E
    slots = count * CAP
    bags = samples * bags_here
    place = lax.axis_index("wa")
    group = lax.axis_index("grp")
    y = (place // 2) % 4
    core = place % 2
    x_low = (place // 8) % 2

    where = jnp.stack([place // 16, y, core, x_low]).astype(I32)

    def moved(step):
        def target(w):
            z, x, yy, c = step(w // 16, (w // 8) % 2, (w // 2) % 4, w % 2)
            return ((z % 8 * 2 + x % 2) * 4 + yy % 4) * 2 + c % 2

        return [(w, target(w)) for w in range(count)]

    to_x = moved(lambda z, x, yy, c: (z, 1 - x, yy, c))
    to_z = [moved(lambda z, x, yy, c, d=d: (z + d, x, yy, c)) for d in range(8)]
    to_peer = [moved(lambda z, x, yy, c, e=e: (z, x, yy + e // 2, c + e % 2)) for e in range(8)]
    groups = [[g * 8 + r for r in range(8)] for g in range(count // 8)]

    live = jnp.arange(depth, dtype=I32) < lengths[0][:, :, None]
    code = jnp.where(live, owners[0] * (1 << ROWS_BITS) + local_rows[0], -1)
    code = jnp.transpose(code, (2, 1, 0)).reshape(depth * bags_here, samples)
    ids, bag, bag_t = call(
        route_kernel,
        (shape((count, CAP), I32), shape((count // 2, 2 * CAP), I32), shape((2 * CAP, count // 2), I32)),
        2 * 4096 * 128 * 1024,
        100000,
    )(code)
    ids_in = lax.all_to_all(ids, "wa", split_axis=0, concat_axis=0, tiled=True)
    tiles = call(
        gather_kernel,
        shape((slots, E), BF16),
        2 * slots * 4096 * E,
        4 << 20,
        [pltpu.VMEM((slots, E), I32), pltpu.VMEM((LOW, table.shape[0] // LOW * E), BF16)],
    )(ids_in, table)
    returned = lax.all_to_all(
        tiles.reshape(count, CAP, E), "wa", split_axis=0, concat_axis=0, tiled=True
    ).reshape(slots, E)
    pooled, part = call(
        pool_kernel,
        (shape((samples, feats), BF16), shape((samples, hidden_width), BF16)),
        2 * slots * 1024 * E + 2 * samples * feats * hidden_width,
        12 << 20,
        [pltpu.VMEM((slots, E), BF16), pltpu.VMEM((LOW, bags // LOW * E), F32)],
    )(bag, bag_t, returned, w_first)
    other = lax.ppermute(part, "grp", [(0, 1), (1, 0)])

    all_pooled = lax.all_gather(pooled, "wa", axis_index_groups=groups, tiled=True)

    width = hidden_width // 8
    logits, head, grad, *pieces = call(
        head_kernel,
        (
            shape((samples, 1), F32),
            shape((1, hidden_width), F32),
            shape((8, samples, width), BF16),
        )
        + (shape((samples, width), BF16),) * 8,
        samples * hidden_width * 60,
        4 << 20,
        placed=4,
    )(where, part, other, labels.reshape(samples, 1), w_head.reshape(1, hidden_width))

    head_share = lax.dynamic_slice_in_dim(head[0], group * (hidden_width // 2), hidden_width // 2)
    head_in = lax.all_to_all(
        head_share.reshape(count, hidden_width // 2 // count), "wa", split_axis=0, concat_axis=0, tiled=True
    )
    head_grad = jnp.sum(head_in, axis=0)

    send = call(
        back_kernel,
        shape((slots, E), BF16),
        2 * slots * 1024 * E + 2 * samples * feats * hidden_width,
        12 << 20,
        [pltpu.VMEM((slots, E), I32), pltpu.VMEM((LOW, bags // LOW * E), BF16)],
    )(grad, w_first, bag_t)
    send, *pieces = lax.optimization_barrier((send, *pieces))
    arrived = lax.all_to_all(
        send.reshape(count, CAP, E), "wa", split_axis=0, concat_axis=0, tiled=True
    ).reshape(slots, E)

    grads = pieces[:1] + [lax.ppermute(pieces[e], "wa", to_peer[e]) for e in range(1, 8)]
    mine, theirs = call(
        dense_kernel,
        (shape((8, feats // 16, width), F32), shape((8, feats // 16, width), BF16)),
        2 * feats * width * 8 * samples,
        8 << 20,
        [pltpu.VMEM((8 * samples, feats), BF16)],
        placed=9,
    )(where, all_pooled, *grads)
    theirs = lax.ppermute(theirs, "wa", to_x)
    block = (feats // 16, width)
    kept, *parts = call(
        cross_kernel, (shape(block, F32),) + (shape(block, BF16),) * 7, 1 << 20, 2 << 20, placed=2
    )(where, mine, theirs)
    parts = [lax.ppermute(parts[d - 1], "wa", to_z[d]) for d in range(1, 8)]
    folded = call(
        fold_kernel, (shape((8, width), F32),) * 8, 1 << 20, 1 << 20, [pltpu.VMEM(block, F32)], placed=8
    )(where, kept, *parts)
    folded = [folded[0]] + [lax.ppermute(folded[e], "wa", to_peer[e]) for e in range(1, 8)]
    dense_grad = call(join_kernel, shape((8, hidden_width), F32), 1 << 16, 1 << 18, placed=8)(where, *folded)

    row_grad = call(
        scatter_kernel,
        shape((table.shape[0], E), BF16),
        2 * slots * 4096 * E,
        4 << 20,
        [pltpu.VMEM((slots, E), BF16), pltpu.VMEM((LOW, table.shape[0] // LOW * E), F32)],
    )(ids_in, ids_in.reshape(count // 2, 2 * CAP), arrived)
    return (logits.reshape(samples), dense_grad, head_grad, row_grad)


def solution(mesh):
    return jax.shard_map(
        shards,
        mesh=mesh,
        in_specs=(
            P(("grp", "wa"), None),
            P("grp", "wa", None, None),
            P("grp", "wa", None, None),
            P("grp", "wa", None),
            P("wa"),
            P("grp", None),
            P(),
        ),
        out_specs=(P("wa"), P(("grp", "wa"), None), P(("grp", "wa")), P(("grp", "wa"), None)),
        check_vma=False,
    )
```

```python
import functools

import jax
import jax.numpy as jnp
from jax import lax
from jax.experimental import pallas as pl
from jax.experimental.pallas import tpu as pltpu
from jax.sharding import PartitionSpec as P

BF16 = jnp.bfloat16
F32 = jnp.float32
I32 = jnp.int32
E = 128
CAP = 64
ROWS_BITS = 12
LOW_BITS = 9
LOW = 1 << LOW_BITS
NT = (((1,), (1,)), ((), ()))


def one_hot(left, right):
    return jnp.where(left == right, 1.0, 0.0).astype(BF16)


def route_kernel(code_ref, ids_ref, bag_ref, bag_t_ref):
    lines = code_ref.shape[0]
    owners = ids_ref.shape[0]
    pairs = owners // 2
    features = lines // 4
    sub = lax.broadcasted_iota(I32, (owners, E), 0)
    half_sub = lax.broadcasted_iota(I32, (CAP, E), 0)
    pair_sub = lax.broadcasted_iota(I32, (pairs, E), 0)
    lane = lax.broadcasted_iota(I32, (1, E), 1)
    before = one_hot(
        jnp.where(lax.broadcasted_iota(I32, (E, E), 0) < lax.broadcasted_iota(I32, (E, E), 1), 1, 0), 1
    )
    named = [jnp.where(sub == code_ref[k : k + 1, :] >> ROWS_BITS, 1.0, 0.0) for k in range(lines)]
    carry = jnp.zeros((owners, 1), F32)
    ids = jnp.zeros((owners, 2 * CAP), F32)
    bag = jnp.zeros((pairs, 2 * E), F32)
    together = 4
    for start in range(0, lines, together):
        owner_parts, place_parts, pair_parts, spot_parts = [], [], [], []
        for k in range(start, start + together):
            code = code_ref[k : k + 1, :]
            owner = code >> ROWS_BITS
            local = code & ((1 << ROWS_BITS) - 1)
            number = (k % features) * E + lane + 1
            named_b = named[k].astype(BF16)
            rank = jnp.dot(named_b, before, preferred_element_type=F32) + carry
            carry = carry + jnp.sum(named[k], axis=1, keepdims=True)
            position = jnp.sum(named[k] * rank, axis=0, keepdims=True).astype(I32)
            place = half_sub == position
            spot = sub == (owner & 1) * CAP + position
            owner_parts.append(named_b)
            place_parts.append(
                jnp.concatenate(
                    [jnp.where(place, (local >> 6).astype(F32), 0.0), jnp.where(place, (local & 63).astype(F32), 0.0)],
                    axis=0,
                ).astype(BF16)
            )
            pair_parts.append(one_hot(pair_sub, owner >> 1))
            spot_parts.append(
                jnp.concatenate(
                    [jnp.where(spot, (number >> 5).astype(F32), 0.0), jnp.where(spot, (number & 31).astype(F32), 0.0)],
                    axis=0,
                ).astype(BF16)
            )
        join = functools.partial(jnp.concatenate, axis=1)
        ids += lax.dot_general(join(owner_parts), join(place_parts), NT, preferred_element_type=F32)
        bag += lax.dot_general(join(pair_parts), join(spot_parts), NT, preferred_element_type=F32)
    ids_ref[...] = (ids[:, :CAP] * 64.0 + ids[:, CAP:]).astype(I32)
    bag = bag[:, :E] * 32.0 + bag[:, E:] - 1.0
    bag_ref[...] = bag.astype(I32)
    bag_t_ref[...] = jnp.transpose(bag).astype(I32)


def spread_columns(lists_t, rows, out_ref):
    for c in range(lists_t.shape[1]):
        out_ref[c * rows : (c + 1) * rows, :] = jnp.broadcast_to(lists_t[:, c : c + 1], (rows, E))


def by_high(data, wide_ref):
    for h in range(data.shape[0] // LOW):
        wide_ref[:, h * E : (h + 1) * E] = data[h * LOW : (h + 1) * LOW, :]


def pick_rows(wanted_ref, wide_ref, out_ref, block):
    lane = lax.broadcasted_iota(I32, (1, E), 1)

    def body(i, _):
        start = pl.multiple_of(i * block, block)
        wanted = wanted_ref[pl.ds(start, block), :]
        low = wanted & (LOW - 1)
        high = wanted >> LOW_BITS
        left = jnp.concatenate([one_hot(low, lane + m * E) for m in range(LOW // E)], axis=1)
        total = jnp.zeros((block, E), F32)
        for h in range(0, wide_ref.shape[1] // E, 2):
            both = jnp.dot(left, wide_ref[:, h * E : (h + 2) * E], preferred_element_type=F32)
            total = jnp.where(high == h, both[:, :E], total)
            total = jnp.where(high == h + 1, both[:, E:], total)
        out_ref[pl.ds(start, block), :] = total.astype(BF16)
        return 0

    lax.fori_loop(0, out_ref.shape[0] // block, body, 0)


def sum_rows(lists_ref, high_ref, data_ref, total_ref):
    chunk = 8
    size = chunk * E
    sub = lax.broadcasted_iota(I32, (LOW, E), 0)
    total_ref[...] = jnp.zeros_like(total_ref)

    def body(i, _):
        start = pl.multiple_of(i * size, size)
        lists = lists_ref[pl.ds(pl.multiple_of(i * chunk, chunk), chunk), :] & (LOW - 1)
        left = jnp.concatenate([one_hot(sub, lists[m : m + 1, :]) for m in range(chunk)], axis=1)
        high = high_ref[pl.ds(start, size), :]
        data = data_ref[pl.ds(start, size), :]
        for h in range(0, total_ref.shape[1] // E, 2):
            right = jnp.concatenate(
                [jnp.where(high == jnp.array(g, BF16), data, jnp.array(0, BF16)) for g in (h, h + 1)], axis=1
            )
            total_ref[:, h * E : (h + 2) * E] += jnp.dot(left, right, preferred_element_type=F32)
        return 0

    lax.fori_loop(0, lists_ref.shape[0] // chunk, body, 0)


def gather_kernel(ids_ref, table_ref, out_ref, spread, wide):
    ids_t = jnp.transpose(ids_ref[...].astype(F32)).astype(I32)
    spread_columns(ids_t, CAP, spread)
    by_high(table_ref, wide)
    pick_rows(spread, wide, out_ref, 1024)


def pool_kernel(bag_ref, bag_t_ref, rows_ref, pooled_ref, high, total):
    samples = pooled_ref.shape[0]
    spread_columns((bag_t_ref[...] >> LOW_BITS).astype(F32).astype(BF16), E, high)
    sum_rows(bag_ref, high, rows_ref, total)
    for f in range(pooled_ref.shape[1] // E):
        h, low = divmod(f * samples, LOW)
        pooled_ref[:, f * E : (f + 1) * E] = total[low : low + samples, h * E : (h + 1) * E].astype(BF16)


def part_kernel(pooled_ref, w_ref, part_ref):
    step = 512
    for j in range(w_ref.shape[1] // step):
        part_ref[:, j * step : (j + 1) * step] = jnp.dot(
            pooled_ref[...], w_ref[:, j * step : (j + 1) * step], preferred_element_type=F32
        )


def peer(where_ref, e, sign):
    return (where_ref[1] + sign * (e // 2) + 4) % 4 * 2 + (where_ref[2] + e % 2) % 2


def head_kernel(
    where_ref, part_ref, pooled_ref, w_near_ref, w_far_ref, labels_ref, w_head_ref,
    logits_ref, head_ref, grad_ref, *rest
):
    piece_refs, total = rest[:-1], rest[-1]
    pieces, samples, width = grad_ref.shape
    half = w_near_ref.shape[0]
    near = pooled_ref[:, pl.ds(pl.multiple_of(where_ref[2] * half, half), half)]
    far = pooled_ref[:, pl.ds(pl.multiple_of((1 - where_ref[2]) * half, half), half)]
    logits = jnp.zeros((samples, 1), F32)
    for q in range(pieces):
        cols = slice(q * width, (q + 1) * width)
        pre = part_ref[:, cols] + (
            jnp.dot(near, w_near_ref[:, cols], preferred_element_type=F32)
            + jnp.dot(far, w_far_ref[:, cols], preferred_element_type=F32)
        )
        total[:, cols] = pre
        hidden = (pre * jax.nn.sigmoid(pre)).astype(BF16).astype(F32)
        logits += jnp.sum(hidden * w_head_ref[:, cols].astype(F32), axis=1, keepdims=True)
    logits_ref[...] = logits
    dlogit = jax.nn.sigmoid(logits) - labels_ref[...]
    for q in range(pieces):
        cols = slice(q * width, (q + 1) * width)
        pre = total[:, cols]
        gate = jax.nn.sigmoid(pre)
        hidden = (pre * gate).astype(BF16).astype(F32)
        head_ref[:, cols] = jnp.sum(hidden * dlogit, axis=0, keepdims=True)
        slope = gate * (1.0 + pre * (1.0 - gate))
        grad_ref[q] = (dlogit * w_head_ref[:, cols].astype(F32) * slope).astype(BF16)
    for e in range(pieces):
        piece_refs[e][...] = grad_ref[peer(where_ref, e, 1)]


def back_kernel(grad_ref, w_ref, bag_t_ref, out_ref, spread, wide):
    pieces, samples, width = grad_ref.shape
    half = w_ref.shape[0] // 2
    spread_columns(bag_t_ref[...], E, spread)
    for h in range(2):
        total = jnp.zeros((samples, half), F32)
        for q in range(pieces):
            total += lax.dot_general(
                grad_ref[q],
                w_ref[h * half : (h + 1) * half, q * width : (q + 1) * width],
                NT,
                preferred_element_type=F32,
            )
        for f in range(half // E):
            high, low = divmod((h * (half // E) + f) * samples, LOW)
            wide[low : low + samples, high * E : (high + 1) * E] = total[:, f * E : (f + 1) * E].astype(BF16)
    pick_rows(spread, wide, out_ref, 1024)


def dense_kernel(where_ref, head_ref, *refs):
    feature_refs, grad_refs, (mine_ref, head_mine_ref, send_ref) = refs[:8], refs[8:16], refs[16:]
    left = jnp.concatenate([r[...] for r in feature_refs], axis=0)
    right = jnp.concatenate([r[...] for r in grad_refs], axis=0)
    half, width = mine_ref.shape[1:]
    planes = mine_ref.shape[0]
    own = where_ref[3] == 0
    share = planes * 2 * E
    head = head_ref[:, pl.ds(pl.multiple_of(where_ref[4] * share, share), share)]
    lines = [head[:, k * E : (k + 1) * E] for k in range(2 * planes)]
    first, second = jnp.concatenate(lines[0::2], axis=0), jnp.concatenate(lines[1::2], axis=0)
    head_mine_ref[...] = jnp.where(own, first, second)
    away = jnp.where(own, second, first)
    high = away.astype(BF16).astype(F32)
    tail = jnp.concatenate([high, away - high], axis=0).astype(BF16)
    send_ref[planes * half :, :] = jnp.concatenate([tail] * (width // E), axis=1)
    for z in range(planes):
        both = lax.dot_general(
            left[:, 2 * half * z : 2 * half * (z + 1)], right, (((0,), (0,)), ((), ())), preferred_element_type=F32
        )
        mine_ref[z] = jnp.where(own, both[:half], both[half:])
        send_ref[z * half : (z + 1) * half, :] = jnp.where(own, both[half:], both[:half]).astype(BF16)


def cross_kernel(mine_ref, head_ref, theirs_ref, out_ref):
    planes, half, width = mine_ref.shape
    rows = half // 8
    tail = theirs_ref[planes * half :, :E].astype(F32)
    head = head_ref[...] + tail[:planes] + tail[planes:]
    high = head.astype(BF16).astype(F32)
    rest = head - high
    empty = jnp.zeros((6, E), F32)
    for z in range(planes):
        block = mine_ref[z] + theirs_ref[z * half : (z + 1) * half, :].astype(F32)
        last = jnp.concatenate([high[z : z + 1], rest[z : z + 1], empty], axis=0)
        parts = []
        for q in range(8):
            parts += [block[q * rows : (q + 1) * rows, m * E : (m + 1) * E] for m in range(width // E)] + [last]
        size = 8 * rows * (width // E + 1)
        out_ref[z * size : (z + 1) * size, :] = jnp.concatenate(parts, axis=0).astype(BF16)


def final_kernel(data_ref, dense_ref, head_ref):
    width = dense_ref.shape[1] // 8
    tiles = width // E
    size = 8 * (tiles + 1)
    head = jnp.zeros((8, E), F32)
    for q in range(0, 8, 2):
        total = jnp.zeros((2 * size, E), F32)
        for z in range(8):
            start = (z * 8 + q) * size
            total += data_ref[start : start + 2 * size, :].astype(F32)
        for n in range(2):
            for m in range(tiles):
                low = n * size + m * 8
                column = (q + n) * width + m * E
                dense_ref[:, column : column + E] = total[low : low + 8]
            head += total[n * size + tiles * 8 : (n + 1) * size]
    head_ref[...] = head[0:1] + head[1:2]


def scatter_kernel(ids_ref, ids2_ref, data_ref, out_ref, high, total):
    ids_t = jnp.transpose((ids_ref[...] >> LOW_BITS).astype(F32)).astype(BF16)
    spread_columns(ids_t, CAP, high)
    sum_rows(ids2_ref, high, data_ref, total)
    for h in range(out_ref.shape[0] // LOW):
        out_ref[h * LOW : (h + 1) * LOW, :] = total[:, h * E : (h + 1) * E].astype(BF16)


def call(kernel, outs, flops, moved, scratch=(), placed=None, mib=16):
    specs = {}
    if placed is not None:
        specs["in_specs"] = [pl.BlockSpec(memory_space=pltpu.SMEM)] + [pl.BlockSpec(memory_space=pltpu.VMEM)] * placed
    return pl.pallas_call(
        kernel,
        out_shape=outs,
        **specs,
        scratch_shapes=list(scratch),
        compiler_params=pltpu.CompilerParams(vmem_limit_bytes=mib << 20),
        cost_estimate=pl.CostEstimate(flops=flops, bytes_accessed=moved, transcendentals=0),
    )


def shape(dims, kind):
    return jax.ShapeDtypeStruct(dims, kind)


def shards(table, owners, local_rows, lengths, labels, w_first, w_head):
    count = lax.axis_size("wa")
    samples = labels.shape[0]
    bags_here = owners.shape[2]
    depth = owners.shape[3]
    hidden_width = w_head.shape[0]
    feats = bags_here * E
    slots = count * CAP
    bags = samples * bags_here
    place = lax.axis_index("wa")
    group = lax.axis_index("grp")
    y = (place // 2) % 4
    core = place % 2
    x_low = (place // 8) % 2

    where = jnp.stack([place // 16, y, core, x_low, group]).astype(I32)

    def moved(step):
        def target(w):
            z, x, yy, c = step(w // 16, (w // 8) % 2, (w // 2) % 4, w % 2)
            return ((z % 8 * 2 + x % 2) * 4 + yy % 4) * 2 + c % 2

        return [(w, target(w)) for w in range(count)]

    to_x = moved(lambda z, x, yy, c: (z, 1 - x, yy, c))
    to_peer = [moved(lambda z, x, yy, c, e=e: (z, x, yy + e // 2, c + e % 2)) for e in range(8)]
    across = [(g * count + w, (1 - g) * count + t) for g in range(2) for w, t in to_x]
    groups = [[z * 16 + x * 8 + r for z in range(8) for r in range(8)] for x in range(2)]

    live = jnp.arange(depth, dtype=I32) < lengths[0][:, :, None]
    code = jnp.where(live, owners[0] * (1 << ROWS_BITS) + local_rows[0], -1)
    code = jnp.transpose(code, (2, 1, 0)).reshape(depth * bags_here, samples)
    ids, bag, bag_t = call(
        route_kernel,
        (shape((count, CAP), I32), shape((count // 2, 2 * CAP), I32), shape((2 * CAP, count // 2), I32)),
        2 * 4096 * 128 * 1024,
        100000,
    )(code)
    ids, w_early = lax.optimization_barrier((ids, w_first))
    near_half = lax.dynamic_slice_in_dim(w_early, core * (feats // 2), feats // 2)
    near_half = lax.ppermute(near_half, ("grp", "wa"), across)
    far_half = lax.ppermute(near_half, "wa", to_peer[1])
    ids_in = lax.all_to_all(ids, "wa", split_axis=0, concat_axis=0, tiled=True)
    tiles = call(
        gather_kernel,
        shape((slots, E), BF16),
        2 * slots * 4096 * E,
        4 << 20,
        [pltpu.VMEM((slots, E), I32), pltpu.VMEM((LOW, table.shape[0] // LOW * E), BF16)],
    )(ids_in, table)
    returned = lax.all_to_all(
        tiles.reshape(count, CAP, E), "wa", split_axis=0, concat_axis=0, tiled=True
    ).reshape(slots, E)
    pooled = call(
        pool_kernel,
        shape((samples, feats), BF16),
        2 * slots * 1024 * E,
        4 << 20,
        [pltpu.VMEM((slots, E), BF16), pltpu.VMEM((LOW, bags // LOW * E), F32)],
    )(bag, bag_t, returned)
    other = lax.ppermute(pooled, "grp", [(0, 1), (1, 0)])
    part = call(
        part_kernel, shape((samples, hidden_width), F32), 2 * samples * feats * hidden_width, 10 << 20, mib=20
    )(pooled, w_first)

    side_pooled = [lax.ppermute(pooled, "wa", to_peer[2 * d]) for d in range(1, 4)]

    width = hidden_width // 8
    logits, head, grad, *pieces = call(
        head_kernel,
        (
            shape((samples, 1), F32),
            shape((1, hidden_width), F32),
            shape((8, samples, width), BF16),
        )
        + (shape((samples, width), BF16),) * 8,
        2 * samples * feats * hidden_width + samples * hidden_width * 60,
        4 << 20,
        [pltpu.VMEM((samples, hidden_width), F32)],
        placed=6,
        mib=24,
    )(where, part, other, near_half, far_half, labels.reshape(samples, 1), w_head.reshape(1, hidden_width))

    grad, *side_pooled = lax.optimization_barrier((grad, *side_pooled))
    all_pooled = []
    for value in [pooled] + side_pooled:
        all_pooled += [value, lax.ppermute(value, "wa", to_peer[1])]

    send = call(
        back_kernel,
        shape((slots, E), BF16),
        2 * slots * 1024 * E + 2 * samples * feats * hidden_width,
        12 << 20,
        [pltpu.VMEM((slots, E), I32), pltpu.VMEM((LOW, bags // LOW * E), BF16)],
        mib=24,
    )(grad, w_first, bag_t)
    send, *pieces = lax.optimization_barrier((send, *pieces))
    arrived = lax.all_to_all(
        send.reshape(count, CAP, E), "wa", split_axis=0, concat_axis=0, tiled=True
    ).reshape(slots, E)

    grads = pieces[:1] + [lax.ppermute(pieces[e], "wa", to_peer[e]) for e in range(1, 8)]
    planes = count // 16
    half = feats // planes // 2
    mine, head_mine, theirs = call(
        dense_kernel,
        (
            shape((planes, half, width), F32),
            shape((planes, E), F32),
            shape((planes * half + 16, width), BF16),
        ),
        2 * feats * width * 8 * samples,
        8 << 20,
        placed=17,
    )(where, head, *all_pooled, *grads)
    theirs = lax.ppermute(theirs, "wa", to_x)
    size = half // 8 * (width // E + 1)
    laid = call(cross_kernel, shape((8 * planes * size, E), BF16), 1 << 20, 2 << 20)(mine, head_mine, theirs)
    other_logits = lax.ppermute(logits, "grp", [(0, 1), (1, 0)])
    laid, ids_pairs, other_logits, arrived = lax.optimization_barrier(
        (laid, ids_in.reshape(count // 2, 2 * CAP), other_logits, arrived)
    )
    blocks = lax.all_to_all(
        laid.reshape(8 * planes, size, E), "wa", 0, 0, axis_index_groups=groups, tiled=True
    ).reshape(8 * planes * size, E)
    dense_grad, head_sums = call(
        final_kernel, (shape((8, hidden_width), F32), shape((1, E), F32)), 1 << 20, 1 << 20
    )(blocks)
    head_grad = lax.dynamic_index_in_dim(head_sums.reshape(8, E // 8), place % 8, 0, False)

    row_grad = call(
        scatter_kernel,
        shape((table.shape[0], E), BF16),
        2 * slots * 4096 * E,
        4 << 20,
        [pltpu.VMEM((slots, E), BF16), pltpu.VMEM((LOW, table.shape[0] // LOW * E), F32)],
    )(ids_in, ids_pairs, arrived)
    logits = jnp.where(group == 0, logits, other_logits)
    return (logits.reshape(samples), dense_grad, head_grad, row_grad)


def solution(mesh):
    return jax.shard_map(
        shards,
        mesh=mesh,
        in_specs=(
            P(("grp", "wa"), None),
            P("grp", "wa", None, None),
            P("grp", "wa", None, None),
            P("grp", "wa", None),
            P("wa"),
            P("grp", None),
            P(),
        ),
        out_specs=(P("wa"), P(("grp", "wa"), None), P(("grp", "wa")), P(("grp", "wa"), None)),
        check_vma=False,
    )
```

```python
import functools

import jax
import jax.numpy as jnp
from jax import lax
from jax.experimental import pallas as pl
from jax.experimental.pallas import tpu as pltpu
from jax.sharding import PartitionSpec as P

BF16 = jnp.bfloat16
F32 = jnp.float32
I32 = jnp.int32
E = 128
CAP = 64
ROWS_BITS = 12
LOW_BITS = 9
LOW = 1 << LOW_BITS
NT = (((1,), (1,)), ((), ()))


def one_hot(left, right):
    return jnp.where(left == right, 1.0, 0.0).astype(BF16)


def route_kernel(where_ref, code_ref, w_ref, ids_ref, bag_ref, bag_t_ref, half_ref, sem):
    rows = half_ref.shape[0]
    copy = pltpu.make_async_copy(w_ref.at[pl.ds(pl.multiple_of(where_ref[2] * rows, rows), rows), :], half_ref, sem)
    copy.start()
    lines = code_ref.shape[0]
    owners = ids_ref.shape[0]
    pairs = owners // 2
    sub = lax.broadcasted_iota(I32, (owners, E), 0)
    half_sub = lax.broadcasted_iota(I32, (CAP, E), 0)
    pair_sub = lax.broadcasted_iota(I32, (pairs, E), 0)
    lane = lax.broadcasted_iota(I32, (1, E), 1)
    before = one_hot(
        jnp.where(lax.broadcasted_iota(I32, (E, E), 0) < lax.broadcasted_iota(I32, (E, E), 1), 1, 0), 1
    )
    named = [jnp.where(sub == code_ref[k : k + 1, :] >> ROWS_BITS, 1.0, 0.0) for k in range(lines)]
    carry = jnp.zeros((owners, 1), F32)
    ids = jnp.zeros((owners, 2 * CAP), F32)
    bag = jnp.zeros((pairs, 2 * E), F32)
    together = 4
    for start in range(0, lines, together):
        owner_parts, place_parts, pair_parts, spot_parts = [], [], [], []
        for k in range(start, start + together):
            code = code_ref[k : k + 1, :]
            owner = code >> ROWS_BITS
            local = code & ((1 << ROWS_BITS) - 1)
            number = (k // 4) * E + lane + 1
            named_b = named[k].astype(BF16)
            rank = jnp.dot(named_b, before, preferred_element_type=F32) + carry
            carry = carry + jnp.sum(named[k], axis=1, keepdims=True)
            position = jnp.sum(named[k] * rank, axis=0, keepdims=True).astype(I32)
            place = half_sub == position
            spot = sub == (owner & 1) * CAP + position
            owner_parts.append(named_b)
            place_parts.append(
                jnp.concatenate(
                    [jnp.where(place, (local >> 6).astype(F32), 0.0), jnp.where(place, (local & 63).astype(F32), 0.0)],
                    axis=0,
                ).astype(BF16)
            )
            pair_parts.append(one_hot(pair_sub, owner >> 1))
            spot_parts.append(
                jnp.concatenate(
                    [jnp.where(spot, (number >> 5).astype(F32), 0.0), jnp.where(spot, (number & 31).astype(F32), 0.0)],
                    axis=0,
                ).astype(BF16)
            )
        join = functools.partial(jnp.concatenate, axis=1)
        ids += lax.dot_general(join(owner_parts), join(place_parts), NT, preferred_element_type=F32)
        bag += lax.dot_general(join(pair_parts), join(spot_parts), NT, preferred_element_type=F32)
    ids = ids[:, :CAP] * 64.0 + ids[:, CAP:]
    ids_ref[...] = jnp.concatenate([ids, ids], axis=1).astype(I32).reshape(ids_ref.shape)
    bag = bag[:, :E] * 32.0 + bag[:, E:] - 1.0
    bag_ref[...] = bag.astype(I32)
    bag_t_ref[...] = jnp.transpose(bag).astype(I32)
    copy.wait()


def spread_columns(lists_t, rows, out_ref):
    for c in range(lists_t.shape[1]):
        out_ref[c * rows : (c + 1) * rows, :] = jnp.broadcast_to(lists_t[:, c : c + 1], (rows, E))


def by_high(data, wide_ref):
    for h in range(data.shape[0] // LOW):
        wide_ref[:, h * E : (h + 1) * E] = data[h * LOW : (h + 1) * LOW, :]


def pick_rows(wanted_ref, wide_ref, out_ref, block):
    lane = lax.broadcasted_iota(I32, (1, E), 1)

    def body(i, _):
        start = pl.multiple_of(i * block, block)
        wanted = wanted_ref[pl.ds(start, block), :]
        low = wanted & (LOW - 1)
        high = wanted >> LOW_BITS
        left = jnp.concatenate([one_hot(low, lane + m * E) for m in range(LOW // E)], axis=1)
        total = jnp.zeros((block, E), F32)
        for h in range(0, wide_ref.shape[1] // E, 2):
            both = jnp.dot(left, wide_ref[:, h * E : (h + 2) * E], preferred_element_type=F32)
            total = jnp.where(high == h, both[:, :E], total)
            total = jnp.where(high == h + 1, both[:, E:], total)
        out_ref[pl.ds(start, block), :] = total.astype(BF16)
        return 0

    lax.fori_loop(0, out_ref.shape[0] // block, body, 0)


def sum_rows(lists, high_ref, data_ref, total_ref):
    chunk = 8
    size = chunk * E
    sub = lax.broadcasted_iota(I32, (LOW, E), 0)
    total_ref[...] = jnp.zeros_like(total_ref)

    def body(i, _):
        start = pl.multiple_of(i * size, size)
        left = jnp.concatenate([one_hot(sub, lists(i * chunk + m) & (LOW - 1)) for m in range(chunk)], axis=1)
        high = high_ref[pl.ds(start, size), :]
        data = data_ref[pl.ds(start, size), :]
        for h in range(0, total_ref.shape[1] // E, 2):
            right = jnp.concatenate(
                [jnp.where(high == jnp.array(g, BF16), data, jnp.array(0, BF16)) for g in (h, h + 1)], axis=1
            )
            total_ref[:, h * E : (h + 2) * E] += jnp.dot(left, right, preferred_element_type=F32)
        return 0

    lax.fori_loop(0, data_ref.shape[0] // size, body, 0)


def gather_kernel(ids_ref, table_ref, out_ref, spread, wide):
    ids = ids_ref[...].reshape(ids_ref.shape[0], 2 * CAP)
    spread_columns(jnp.transpose(ids.astype(F32)).astype(I32)[:CAP], CAP, spread)
    by_high(table_ref, wide)
    pick_rows(spread, wide, out_ref, 1024)


def pool_kernel(bag_ref, bag_t_ref, rows_ref, pooled_ref, high, total):
    samples = pooled_ref.shape[0]
    spread_columns((bag_t_ref[...] >> LOW_BITS).astype(F32).astype(BF16), E, high)
    sum_rows(lambda k: bag_ref[pl.ds(k, 1), :], high, rows_ref, total)
    for f in range(pooled_ref.shape[1] // E):
        h, low = divmod(f * samples, LOW)
        pooled_ref[:, f * E : (f + 1) * E] = total[low : low + samples, h * E : (h + 1) * E].astype(BF16)


def part_kernel(pooled_ref, w_ref, part_ref):
    step = 512
    for j in range(w_ref.shape[1] // step):
        part_ref[:, j * step : (j + 1) * step] = jnp.dot(
            pooled_ref[...], w_ref[:, j * step : (j + 1) * step], preferred_element_type=F32
        )


def peer(where_ref, e, sign):
    return (where_ref[1] + sign * (e // 2) + 4) % 4 * 2 + (where_ref[2] + e % 2) % 2


def head_kernel(
    where_ref, part_ref, pooled_ref, w_near_ref, w_far_ref, labels_ref, w_head_ref,
    logits_ref, head_ref, grad_ref, away_ref, *rest
):
    piece_refs, total = rest[:-1], rest[-1]
    pieces, samples, width = grad_ref.shape
    half = w_near_ref.shape[0]
    near = pooled_ref[:, pl.ds(pl.multiple_of(where_ref[2] * half, half), half)]
    far = pooled_ref[:, pl.ds(pl.multiple_of((1 - where_ref[2]) * half, half), half)]
    logits = jnp.zeros((samples, 1), F32)
    for q in range(pieces):
        cols = slice(q * width, (q + 1) * width)
        pre = part_ref[:, cols] + (
            jnp.dot(near, w_near_ref[:, cols], preferred_element_type=F32)
            + jnp.dot(far, w_far_ref[:, cols], preferred_element_type=F32)
        )
        total[:, cols] = pre
        hidden = (pre * jax.nn.sigmoid(pre)).astype(BF16).astype(F32)
        logits += jnp.sum(hidden * w_head_ref[:, cols].astype(F32), axis=1, keepdims=True)
    logits_ref[...] = logits
    dlogit = jax.nn.sigmoid(logits) - labels_ref[...]
    for q in range(pieces):
        cols = slice(q * width, (q + 1) * width)
        pre = total[:, cols]
        gate = jax.nn.sigmoid(pre)
        hidden = (pre * gate).astype(BF16).astype(F32)
        head_ref[:, cols] = jnp.sum(hidden * dlogit, axis=0, keepdims=True)
        slope = gate * (1.0 + pre * (1.0 - gate))
        grad_ref[q] = (dlogit * w_head_ref[:, cols].astype(F32) * slope).astype(BF16)
    for d in range(pieces // 2):
        piece_refs[d][...] = grad_ref[peer(where_ref, 2 * d, 1)]
        away_ref[d] = grad_ref[peer(where_ref, 2 * d + 1, 1)]


def pack_kernel(near_ref, *refs):
    for d in range(3):
        samples = near_ref.shape[1]
        refs[3 + d][:samples, :] = refs[d][...]
        refs[3 + d][samples:, :] = near_ref[d + 1]


def back_kernel(grad_ref, w_ref, bag_t_ref, out_ref, spread, wide):
    pieces, samples, width = grad_ref.shape
    half = w_ref.shape[0] // 2
    spread_columns(bag_t_ref[...], E, spread)
    for h in range(2):
        total = jnp.zeros((samples, half), F32)
        for q in range(pieces):
            total += lax.dot_general(
                grad_ref[q],
                w_ref[h * half : (h + 1) * half, q * width : (q + 1) * width],
                NT,
                preferred_element_type=F32,
            )
        for f in range(half // E):
            high, low = divmod((h * (half // E) + f) * samples, LOW)
            wide[low : low + samples, high * E : (high + 1) * E] = total[:, f * E : (f + 1) * E].astype(BF16)
    pick_rows(spread, wide, out_ref, 1024)


def dense_kernel(where_ref, head_ref, *refs):
    feature_refs, grad_refs, (mine_ref, head_mine_ref, send_ref) = refs[:8], refs[8:13], refs[13:]
    left = jnp.concatenate([r[...] for r in feature_refs], axis=0)
    right = jnp.concatenate([grad_refs[0][...], grad_refs[1][0]] + [r[...] for r in grad_refs[2:]], axis=0)
    half, width = mine_ref.shape[1:]
    planes = mine_ref.shape[0]
    own = where_ref[3] == 0
    share = planes * 2 * E
    head = head_ref[:, pl.ds(pl.multiple_of(where_ref[4] * share, share), share)]
    lines = [head[:, k * E : (k + 1) * E] for k in range(2 * planes)]
    first, second = jnp.concatenate(lines[0::2], axis=0), jnp.concatenate(lines[1::2], axis=0)
    head_mine_ref[...] = jnp.where(own, first, second)
    away = jnp.where(own, second, first)
    high = away.astype(BF16).astype(F32)
    tail = jnp.concatenate([high, away - high], axis=0).astype(BF16)
    send_ref[planes * half :, :] = jnp.concatenate([tail] * (width // E), axis=1)
    for z in range(planes):
        both = lax.dot_general(
            left[:, 2 * half * z : 2 * half * (z + 1)], right, (((0,), (0,)), ((), ())), preferred_element_type=F32
        )
        mine_ref[z] = jnp.where(own, both[:half], both[half:])
        send_ref[z * half : (z + 1) * half, :] = jnp.where(own, both[half:], both[:half]).astype(BF16)


def cross_kernel(mine_ref, head_ref, theirs_ref, out_ref):
    planes, half, width = mine_ref.shape
    rows = half // 8
    tail = theirs_ref[planes * half :, :E].astype(F32)
    head = head_ref[...] + tail[:planes] + tail[planes:]
    high = head.astype(BF16).astype(F32)
    rest = head - high
    empty = jnp.zeros((6, E), F32)
    for z in range(planes):
        block = mine_ref[z] + theirs_ref[z * half : (z + 1) * half, :].astype(F32)
        last = jnp.concatenate([high[z : z + 1], rest[z : z + 1], empty], axis=0)
        parts = []
        for q in range(8):
            parts += [block[q * rows : (q + 1) * rows, m * E : (m + 1) * E] for m in range(width // E)] + [last]
        size = 8 * rows * (width // E + 1)
        out_ref[z * size : (z + 1) * size, :] = jnp.concatenate(parts, axis=0).astype(BF16)


def final_kernel(data_ref, dense_ref, head_ref):
    width = dense_ref.shape[1] // 8
    tiles = width // E
    size = 8 * (tiles + 1)
    head = jnp.zeros((8, E), F32)
    for q in range(0, 8, 2):
        total = jnp.zeros((2 * size, E), F32)
        for z in range(8):
            start = (z * 8 + q) * size
            total += data_ref[start : start + 2 * size, :].astype(F32)
        for n in range(2):
            for m in range(tiles):
                low = n * size + m * 8
                column = (q + n) * width + m * E
                dense_ref[:, column : column + E] = total[low : low + 8]
            head += total[n * size + tiles * 8 : (n + 1) * size]
    head_ref[...] = head[0:1] + head[1:2]


def scatter_kernel(ids_ref, data_ref, out_ref, high, total):
    ids = ids_ref[...].reshape(ids_ref.shape[0], 2 * CAP)
    spread_columns(jnp.transpose((ids >> LOW_BITS).astype(F32))[:CAP].astype(BF16), CAP, high)
    first = lax.broadcasted_iota(I32, (1, E), 1) < CAP

    def lists(k):
        return jnp.where(first, ids_ref[2 * k], ids_ref[2 * k + 1])

    sum_rows(lists, high, data_ref, total)
    for h in range(out_ref.shape[0] // LOW):
        out_ref[h * LOW : (h + 1) * LOW, :] = total[:, h * E : (h + 1) * E].astype(BF16)


def call(kernel, outs, flops, moved, scratch=(), placed=None, mib=16, in_specs=None):
    specs = {} if in_specs is None else {"in_specs": in_specs}
    if placed is not None:
        specs["in_specs"] = [pl.BlockSpec(memory_space=pltpu.SMEM)] + [pl.BlockSpec(memory_space=pltpu.VMEM)] * placed
    return pl.pallas_call(
        kernel,
        out_shape=outs,
        **specs,
        scratch_shapes=list(scratch),
        compiler_params=pltpu.CompilerParams(vmem_limit_bytes=mib << 20),
        cost_estimate=pl.CostEstimate(flops=flops, bytes_accessed=moved, transcendentals=0),
    )


def shape(dims, kind):
    return jax.ShapeDtypeStruct(dims, kind)


def shards(table, owners, local_rows, lengths, labels, w_first, w_head):
    count = lax.axis_size("wa")
    samples = labels.shape[0]
    bags_here = owners.shape[2]
    depth = owners.shape[3]
    hidden_width = w_head.shape[0]
    feats = bags_here * E
    slots = count * CAP
    bags = samples * bags_here
    place = lax.axis_index("wa")
    group = lax.axis_index("grp")
    y = (place // 2) % 4
    core = place % 2
    x_low = (place // 8) % 2

    where = jnp.stack([place // 16, y, core, x_low, group]).astype(I32)

    def moved(step):
        def target(w):
            z, x, yy, c = step(w // 16, (w // 8) % 2, (w // 2) % 4, w % 2)
            return ((z % 8 * 2 + x % 2) * 4 + yy % 4) * 2 + c % 2

        return [(w, target(w)) for w in range(count)]

    to_x = moved(lambda z, x, yy, c: (z, 1 - x, yy, c))
    to_peer = [moved(lambda z, x, yy, c, e=e: (z, x, yy + e // 2, c + e % 2)) for e in range(8)]
    across = [(g * count + w, (1 - g) * count + t) for g in range(2) for w, t in to_x]
    groups = [[z * 16 + x * 8 + r for z in range(8) for r in range(8)] for x in range(2)]

    small, vmem, far = (pl.BlockSpec(memory_space=m) for m in (pltpu.SMEM, pltpu.VMEM, pltpu.HBM))
    live = jnp.arange(depth, dtype=I32) < lengths[0][:, :, None]
    code = jnp.where(live, owners[0] * (1 << ROWS_BITS) + local_rows[0], -1)
    code = jnp.transpose(code, (1, 2, 0)).reshape(bags_here * depth, samples)
    ids, bag, bag_t, near_half = pl.pallas_call(
        route_kernel,
        out_shape=(
            shape((count, 1, 2 * CAP), I32),
            shape((count // 2, 2 * CAP), I32),
            shape((2 * CAP, count // 2), I32),
            shape((feats // 2, hidden_width), BF16),
        ),
        in_specs=[small, vmem, far],
        out_specs=[vmem] * 4,
        scratch_shapes=[pltpu.SemaphoreType.DMA],
        compiler_params=pltpu.CompilerParams(vmem_limit_bytes=58 << 20),
        cost_estimate=pl.CostEstimate(flops=1 << 30, bytes_accessed=8 << 20, transcendentals=0),
    )(where, code, w_first)
    near_half = lax.ppermute(near_half, ("grp", "wa"), across)
    far_half = lax.ppermute(near_half, "wa", to_peer[1])
    ids_in = lax.all_to_all(ids, "wa", split_axis=0, concat_axis=0, tiled=True)
    tiles = call(
        gather_kernel,
        shape((slots, E), BF16),
        2 * slots * 4096 * E,
        4 << 20,
        [pltpu.VMEM((slots, E), I32), pltpu.VMEM((LOW, table.shape[0] // LOW * E), BF16)],
    )(ids_in, table)
    returned = lax.all_to_all(
        tiles.reshape(count, CAP, E), "wa", split_axis=0, concat_axis=0, tiled=True
    ).reshape(slots, E)
    pooled = call(
        pool_kernel,
        shape((samples, feats), BF16),
        2 * slots * 1024 * E,
        4 << 20,
        [pltpu.VMEM((slots, E), BF16), pltpu.VMEM((LOW, bags // LOW * E), F32)],
    )(bag, bag_t, returned)
    other = lax.ppermute(pooled, "grp", [(0, 1), (1, 0)])
    part = call(
        part_kernel, shape((samples, hidden_width), F32), 2 * samples * feats * hidden_width, 10 << 20, mib=20
    )(pooled, w_first)

    side_pooled = [lax.ppermute(pooled, "wa", to_peer[2 * d]) for d in range(1, 4)]

    width = hidden_width // 8
    logits, head, grad, away, *pieces = call(
        head_kernel,
        (
            shape((samples, 1), F32),
            shape((1, hidden_width), F32),
            shape((8, samples, width), BF16),
            shape((4, samples, width), BF16),
        )
        + (shape((samples, width), BF16),) * 4,
        2 * samples * feats * hidden_width + samples * hidden_width * 60,
        4 << 20,
        [pltpu.VMEM((samples, hidden_width), F32)],
        placed=6,
        mib=24,
    )(where, part, other, near_half, far_half, labels.reshape(samples, 1), w_head.reshape(1, hidden_width))

    grad, *side_pooled = lax.optimization_barrier((grad, *side_pooled))
    all_pooled = []
    for value in [pooled] + side_pooled:
        all_pooled += [value, lax.ppermute(value, "wa", to_peer[1])]

    send = call(
        back_kernel,
        shape((slots, E), BF16),
        2 * slots * 1024 * E + 2 * samples * feats * hidden_width,
        12 << 20,
        [pltpu.VMEM((slots, E), I32), pltpu.VMEM((LOW, bags // LOW * E), BF16)],
        mib=24,
    )(grad, w_first, bag_t)
    near = lax.ppermute(away, "wa", to_peer[1])
    send, near, *pieces = lax.optimization_barrier((send, near, *pieces))
    arrived = lax.all_to_all(
        send.reshape(count, CAP, E), "wa", split_axis=0, concat_axis=0, tiled=True
    ).reshape(slots, E)

    packed = call(pack_kernel, (shape((2 * samples, width), BF16),) * 3, 1 << 16, 1 << 20)(near, *pieces[1:])
    grads = [pieces[0], near] + [lax.ppermute(packed[d - 1], "wa", to_peer[2 * d]) for d in range(1, 4)]
    planes = count // 16
    half = feats // planes // 2
    mine, head_mine, theirs = call(
        dense_kernel,
        (
            shape((planes, half, width), F32),
            shape((planes, E), F32),
            shape((planes * half + 16, width), BF16),
        ),
        2 * feats * width * 8 * samples,
        8 << 20,
        placed=14,
    )(where, head, *all_pooled, *grads)
    theirs = lax.ppermute(theirs, "wa", to_x)
    size = half // 8 * (width // E + 1)
    laid = call(cross_kernel, shape((8 * planes * size, E), BF16), 1 << 20, 2 << 20)(mine, head_mine, theirs)
    other_logits = lax.ppermute(logits, "grp", [(0, 1), (1, 0)])
    laid, other_logits, arrived = lax.optimization_barrier((laid, other_logits, arrived))
    blocks = lax.all_to_all(
        laid.reshape(8 * planes, size, E), "wa", 0, 0, axis_index_groups=groups, tiled=True
    ).reshape(8 * planes * size, E)
    dense_grad, head_sums = call(
        final_kernel, (shape((8, hidden_width), F32), shape((1, E), F32)), 1 << 20, 1 << 20
    )(blocks)
    head_grad = lax.dynamic_index_in_dim(head_sums.reshape(8, E // 8), place % 8, 0, False)

    row_grad = call(
        scatter_kernel,
        shape((table.shape[0], E), BF16),
        2 * slots * 4096 * E,
        4 << 20,
        [pltpu.VMEM((slots, E), BF16), pltpu.VMEM((LOW, table.shape[0] // LOW * E), F32)],
    )(ids_in, arrived)
    logits = jnp.where(group == 0, logits, other_logits)
    return (logits.reshape(samples), dense_grad, head_grad, row_grad)


def solution(mesh):
    return jax.shard_map(
        shards,
        mesh=mesh,
        in_specs=(
            P(("grp", "wa"), None),
            P("grp", "wa", None, None),
            P("grp", "wa", None, None),
            P("grp", "wa", None),
            P("wa"),
            P("grp", None),
            P(),
        ),
        out_specs=(P("wa"), P(("grp", "wa"), None), P(("grp", "wa")), P(("grp", "wa"), None)),
        check_vma=False,
    )
```

```python
import functools

import jax
import jax.numpy as jnp
from jax import lax
from jax.experimental import pallas as pl
from jax.experimental.pallas import tpu as pltpu
from jax.sharding import PartitionSpec as P

BF16 = jnp.bfloat16
F32 = jnp.float32
I32 = jnp.int32
E = 128
CAP = 64
ROWS_BITS = 12
LOW_BITS = 9
LOW = 1 << LOW_BITS
NT = (((1,), (1,)), ((), ()))


def one_hot(left, right):
    return jnp.where(left == right, 1.0, 0.0).astype(BF16)


def route_kernel(code_ref, w_ref, ids_ref, bag_ref, bag_t_ref, half_ref, sem):
    rows = half_ref.shape[0]
    start = pl.multiple_of(lax.axis_index("wa") % 2 * rows, rows)
    copy = pltpu.make_async_copy(w_ref.at[pl.ds(start, rows), :], half_ref, sem)
    copy.start()
    lines = code_ref.shape[0]
    owners = ids_ref.shape[0]
    pairs = owners // 2
    sub = lax.broadcasted_iota(I32, (owners, E), 0)
    half_sub = lax.broadcasted_iota(I32, (CAP, E), 0)
    pair_sub = lax.broadcasted_iota(I32, (pairs, E), 0)
    lane = lax.broadcasted_iota(I32, (1, E), 1)
    before = one_hot(
        jnp.where(lax.broadcasted_iota(I32, (E, E), 0) < lax.broadcasted_iota(I32, (E, E), 1), 1, 0), 1
    )
    named = [jnp.where(sub == code_ref[k : k + 1, :] >> ROWS_BITS, 1.0, 0.0) for k in range(lines)]
    carry = jnp.zeros((owners, 1), F32)
    ids = jnp.zeros((owners, 2 * CAP), F32)
    bag = jnp.zeros((pairs, 2 * E), F32)
    together = 4
    for start in range(0, lines, together):
        owner_parts, place_parts, pair_parts, spot_parts = [], [], [], []
        for k in range(start, start + together):
            code = code_ref[k : k + 1, :]
            owner = code >> ROWS_BITS
            local = code & ((1 << ROWS_BITS) - 1)
            number = (k // 4) * E + lane + 1
            named_b = named[k].astype(BF16)
            rank = jnp.dot(named_b, before, preferred_element_type=F32) + carry
            carry = carry + jnp.sum(named[k], axis=1, keepdims=True)
            position = jnp.sum(named[k] * rank, axis=0, keepdims=True).astype(I32)
            place = half_sub == position
            spot = sub == (owner & 1) * CAP + position
            owner_parts.append(named_b)
            place_parts.append(
                jnp.concatenate(
                    [jnp.where(place, (local >> 6).astype(F32), 0.0), jnp.where(place, (local & 63).astype(F32), 0.0)],
                    axis=0,
                ).astype(BF16)
            )
            pair_parts.append(one_hot(pair_sub, owner >> 1))
            spot_parts.append(
                jnp.concatenate(
                    [jnp.where(spot, (number >> 5).astype(F32), 0.0), jnp.where(spot, (number & 31).astype(F32), 0.0)],
                    axis=0,
                ).astype(BF16)
            )
        join = functools.partial(jnp.concatenate, axis=1)
        ids += lax.dot_general(join(owner_parts), join(place_parts), NT, preferred_element_type=F32)
        bag += lax.dot_general(join(pair_parts), join(spot_parts), NT, preferred_element_type=F32)
    ids = ids[:, :CAP] * 64.0 + ids[:, CAP:]
    ids_ref[...] = jnp.concatenate([ids, ids], axis=1).astype(I32).reshape(ids_ref.shape)
    bag = bag[:, :E] * 32.0 + bag[:, E:] - 1.0
    bag_ref[...] = bag.astype(I32)
    bag_t_ref[...] = jnp.transpose(bag).astype(I32)
    copy.wait()


def spread_columns(lists_t, rows, out_ref):
    for c in range(lists_t.shape[1]):
        out_ref[c * rows : (c + 1) * rows, :] = jnp.broadcast_to(lists_t[:, c : c + 1], (rows, E))


def by_high(data, wide_ref):
    for h in range(data.shape[0] // LOW):
        wide_ref[:, h * E : (h + 1) * E] = data[h * LOW : (h + 1) * LOW, :]


def pick_rows(wanted_ref, wide_ref, out_ref, block):
    lane = lax.broadcasted_iota(I32, (1, E), 1)

    def body(i, _):
        start = pl.multiple_of(i * block, block)
        wanted = wanted_ref[pl.ds(start, block), :]
        low = wanted & (LOW - 1)
        high = wanted >> LOW_BITS
        left = jnp.concatenate([one_hot(low, lane + m * E) for m in range(LOW // E)], axis=1)
        total = jnp.zeros((block, E), F32)
        for h in range(0, wide_ref.shape[1] // E, 2):
            both = jnp.dot(left, wide_ref[:, h * E : (h + 2) * E], preferred_element_type=F32)
            total = jnp.where(high == h, both[:, :E], total)
            total = jnp.where(high == h + 1, both[:, E:], total)
        out_ref[pl.ds(start, block), :] = total.astype(BF16)
        return 0

    lax.fori_loop(0, out_ref.shape[0] // block, body, 0, unroll=True)


def sum_rows(lists, high_ref, data_ref, total_ref):
    chunk = 8
    size = chunk * E
    sub = lax.broadcasted_iota(I32, (LOW, E), 0)
    total_ref[...] = jnp.zeros_like(total_ref)

    def body(i, _):
        start = pl.multiple_of(i * size, size)
        left = jnp.concatenate([one_hot(sub, lists(i * chunk + m) & (LOW - 1)) for m in range(chunk)], axis=1)
        high = high_ref[pl.ds(start, size), :]
        data = data_ref[pl.ds(start, size), :]
        for h in range(0, total_ref.shape[1] // E, 2):
            right = jnp.concatenate(
                [jnp.where(high == jnp.array(g, BF16), data, jnp.array(0, BF16)) for g in (h, h + 1)], axis=1
            )
            total_ref[:, h * E : (h + 2) * E] += jnp.dot(left, right, preferred_element_type=F32)
        return 0

    lax.fori_loop(0, data_ref.shape[0] // size, body, 0, unroll=4)


def gather_kernel(ids_ref, table_ref, out_ref, spread, wide):
    ids = ids_ref[...].reshape(ids_ref.shape[0], 2 * CAP)
    spread_columns(jnp.transpose(ids.astype(F32)).astype(I32)[:CAP], CAP, spread)
    by_high(table_ref, wide)
    pick_rows(spread, wide, out_ref, 1024)


def pool_kernel(bag_ref, bag_t_ref, rows_ref, pooled_ref, high, total):
    samples = pooled_ref.shape[0]
    spread_columns((bag_t_ref[...] >> LOW_BITS).astype(F32).astype(BF16), E, high)
    sum_rows(lambda k: bag_ref[pl.ds(k, 1), :], high, rows_ref, total)
    for f in range(pooled_ref.shape[1] // E):
        h, low = divmod(f * samples, LOW)
        pooled_ref[:, f * E : (f + 1) * E] = total[low : low + samples, h * E : (h + 1) * E].astype(BF16)


def part_kernel(pooled_ref, w_ref, part_ref):
    step = 512
    for j in range(w_ref.shape[1] // step):
        part_ref[:, j * step : (j + 1) * step] = jnp.dot(
            pooled_ref[...], w_ref[:, j * step : (j + 1) * step], preferred_element_type=F32
        )


def peer(where_ref, e, sign):
    return (where_ref[1] + sign * (e // 2) + 4) % 4 * 2 + (where_ref[2] + e % 2) % 2


def head_kernel(
    where_ref, part_ref, pooled_ref, w_near_ref, w_far_ref, labels_ref, w_head_ref,
    logits_ref, head_ref, grad_ref, away_ref, *rest
):
    piece_refs, total = rest[:-1], rest[-1]
    pieces, samples, width = grad_ref.shape
    half = w_near_ref.shape[0]
    near = pooled_ref[:, pl.ds(pl.multiple_of(where_ref[2] * half, half), half)]
    far = pooled_ref[:, pl.ds(pl.multiple_of((1 - where_ref[2]) * half, half), half)]
    logits = jnp.zeros((samples, 1), F32)
    for q in range(pieces):
        cols = slice(q * width, (q + 1) * width)
        pre = part_ref[:, cols] + (
            jnp.dot(near, w_near_ref[:, cols], preferred_element_type=F32)
            + jnp.dot(far, w_far_ref[:, cols], preferred_element_type=F32)
        )
        total[:, cols] = pre
        hidden = (pre * jax.nn.sigmoid(pre)).astype(BF16).astype(F32)
        logits += jnp.sum(hidden * w_head_ref[:, cols].astype(F32), axis=1, keepdims=True)
    logits_ref[...] = logits
    dlogit = jax.nn.sigmoid(logits) - labels_ref[...]
    for q in range(pieces):
        cols = slice(q * width, (q + 1) * width)
        pre = total[:, cols]
        gate = jax.nn.sigmoid(pre)
        hidden = (pre * gate).astype(BF16).astype(F32)
        head_ref[:, cols] = jnp.sum(hidden * dlogit, axis=0, keepdims=True)
        slope = gate * (1.0 + pre * (1.0 - gate))
        grad_ref[q] = (dlogit * w_head_ref[:, cols].astype(F32) * slope).astype(BF16)
    for d in range(pieces // 2):
        piece_refs[d][...] = grad_ref[peer(where_ref, 2 * d, 1)]
        away_ref[d] = grad_ref[peer(where_ref, 2 * d + 1, 1)]


def pack_kernel(near_ref, *refs):
    for d in range(3):
        samples = near_ref.shape[1]
        refs[3 + d][:samples, :] = refs[d][...]
        refs[3 + d][samples:, :] = near_ref[d + 1]


def back_kernel(grad_ref, w_ref, bag_t_ref, out_ref, spread, wide):
    pieces, samples, width = grad_ref.shape
    half = w_ref.shape[0] // 2
    spread_columns(bag_t_ref[...], E, spread)
    for h in range(2):
        total = jnp.zeros((samples, half), F32)
        for q in range(pieces):
            total += lax.dot_general(
                grad_ref[q],
                w_ref[h * half : (h + 1) * half, q * width : (q + 1) * width],
                NT,
                preferred_element_type=F32,
            )
        for f in range(half // E):
            high, low = divmod((h * (half // E) + f) * samples, LOW)
            wide[low : low + samples, high * E : (high + 1) * E] = total[:, f * E : (f + 1) * E].astype(BF16)
    pick_rows(spread, wide, out_ref, 1024)


def stack_kernel(*refs):
    for e, ref in enumerate(refs[:-1]):
        rows = ref.shape[0]
        refs[-1][e * rows : (e + 1) * rows, :] = ref[...]


def dense_kernel(where_ref, head_ref, *refs):
    left_ref, grad_refs, (mine_ref, head_mine_ref, send_ref) = refs[0], refs[1:6], refs[6:]
    right = jnp.concatenate([grad_refs[0][...], grad_refs[1][0]] + [r[...] for r in grad_refs[2:]], axis=0)
    half, width = mine_ref.shape[1:]
    planes = mine_ref.shape[0]
    own = where_ref[3] == 0
    share = planes * 2 * E
    head = head_ref[:, pl.ds(pl.multiple_of(where_ref[4] * share, share), share)]
    lines = [head[:, k * E : (k + 1) * E] for k in range(2 * planes)]
    first, second = jnp.concatenate(lines[0::2], axis=0), jnp.concatenate(lines[1::2], axis=0)
    head_mine_ref[...] = jnp.where(own, first, second)
    away = jnp.where(own, second, first)
    high = away.astype(BF16).astype(F32)
    tail = jnp.concatenate([high, away - high], axis=0).astype(BF16)
    send_ref[planes * half :, :] = jnp.concatenate([tail] * (width // E), axis=1)
    for z in range(planes):
        both = lax.dot_general(
            left_ref[:, 2 * half * z : 2 * half * (z + 1)], right, (((0,), (0,)), ((), ())), preferred_element_type=F32
        )
        mine_ref[z] = jnp.where(own, both[:half], both[half:])
        send_ref[z * half : (z + 1) * half, :] = jnp.where(own, both[half:], both[:half]).astype(BF16)


def cross_kernel(mine_ref, head_ref, theirs_ref, out_ref):
    planes, half, width = mine_ref.shape
    rows = half // 8
    tail = theirs_ref[planes * half :, :E].astype(F32)
    head = head_ref[...] + tail[:planes] + tail[planes:]
    high = head.astype(BF16).astype(F32)
    rest = head - high
    empty = jnp.zeros((6, E), F32)
    for z in range(planes):
        block = mine_ref[z] + theirs_ref[z * half : (z + 1) * half, :].astype(F32)
        last = jnp.concatenate([high[z : z + 1], rest[z : z + 1], empty], axis=0)
        parts = []
        for q in range(8):
            parts += [block[q * rows : (q + 1) * rows, m * E : (m + 1) * E] for m in range(width // E)] + [last]
        size = 8 * rows * (width // E + 1)
        out_ref[z * size : (z + 1) * size, :] = jnp.concatenate(parts, axis=0).astype(BF16)


def final_kernel(data_ref, dense_ref, head_ref):
    width = dense_ref.shape[1] // 8
    tiles = width // E
    size = 8 * (tiles + 1)
    head = jnp.zeros((8, E), F32)
    for q in range(0, 8, 2):
        total = jnp.zeros((2 * size, E), F32)
        for z in range(8):
            start = (z * 8 + q) * size
            total += data_ref[start : start + 2 * size, :].astype(F32)
        for n in range(2):
            for m in range(tiles):
                low = n * size + m * 8
                column = (q + n) * width + m * E
                dense_ref[:, column : column + E] = total[low : low + 8]
            head += total[n * size + tiles * 8 : (n + 1) * size]
    head_ref[...] = head[0:1] + head[1:2]


def scatter_kernel(ids_ref, data_ref, out_ref, high, total):
    ids = ids_ref[...].reshape(ids_ref.shape[0], 2 * CAP)
    spread_columns(jnp.transpose((ids >> LOW_BITS).astype(F32))[:CAP].astype(BF16), CAP, high)
    first = lax.broadcasted_iota(I32, (1, E), 1) < CAP

    def lists(k):
        return jnp.where(first, ids_ref[2 * k], ids_ref[2 * k + 1])

    sum_rows(lists, high, data_ref, total)
    for h in range(out_ref.shape[0] // LOW):
        out_ref[h * LOW : (h + 1) * LOW, :] = total[:, h * E : (h + 1) * E].astype(BF16)


def call(kernel, outs, flops, moved, scratch=(), placed=None, mib=16, in_specs=None):
    specs = {} if in_specs is None else {"in_specs": in_specs}
    if placed is not None:
        specs["in_specs"] = [pl.BlockSpec(memory_space=pltpu.SMEM)] + [pl.BlockSpec(memory_space=pltpu.VMEM)] * placed
    return pl.pallas_call(
        kernel,
        out_shape=outs,
        **specs,
        scratch_shapes=list(scratch),
        compiler_params=pltpu.CompilerParams(vmem_limit_bytes=mib << 20),
        cost_estimate=pl.CostEstimate(flops=flops, bytes_accessed=moved, transcendentals=0),
    )


def shape(dims, kind):
    return jax.ShapeDtypeStruct(dims, kind)


def shards(table, owners, local_rows, lengths, labels, w_first, w_head):
    count = lax.axis_size("wa")
    samples = labels.shape[0]
    bags_here = owners.shape[2]
    depth = owners.shape[3]
    hidden_width = w_head.shape[0]
    feats = bags_here * E
    slots = count * CAP
    bags = samples * bags_here
    place = lax.axis_index("wa")
    group = lax.axis_index("grp")
    y = (place // 2) % 4
    core = place % 2
    x_low = (place // 8) % 2

    where = jnp.stack([place // 16, y, core, x_low, group]).astype(I32)

    def moved(step):
        def target(w):
            z, x, yy, c = step(w // 16, (w // 8) % 2, (w // 2) % 4, w % 2)
            return ((z % 8 * 2 + x % 2) * 4 + yy % 4) * 2 + c % 2

        return [(w, target(w)) for w in range(count)]

    to_x = moved(lambda z, x, yy, c: (z, 1 - x, yy, c))
    to_peer = [moved(lambda z, x, yy, c, e=e: (z, x, yy + e // 2, c + e % 2)) for e in range(8)]
    across = [(g * count + w, (1 - g) * count + t) for g in range(2) for w, t in to_x]
    groups = [[z * 16 + x * 8 + r for z in range(8) for r in range(8)] for x in range(2)]

    small, vmem, far = (pl.BlockSpec(memory_space=m) for m in (pltpu.SMEM, pltpu.VMEM, pltpu.HBM))
    live = jnp.arange(depth, dtype=I32) < lengths[0][:, :, None]
    code = jnp.where(live, owners[0] * (1 << ROWS_BITS) + local_rows[0], -1)
    code = jnp.transpose(code, (1, 2, 0)).reshape(bags_here * depth, samples)
    ids, bag, bag_t, near_half = pl.pallas_call(
        route_kernel,
        out_shape=(
            shape((count, 1, 2 * CAP), I32),
            shape((count // 2, 2 * CAP), I32),
            shape((2 * CAP, count // 2), I32),
            shape((feats // 2, hidden_width), BF16),
        ),
        in_specs=[vmem, far],
        out_specs=[vmem] * 4,
        scratch_shapes=[pltpu.SemaphoreType.DMA],
        compiler_params=pltpu.CompilerParams(vmem_limit_bytes=58 << 20),
        cost_estimate=pl.CostEstimate(flops=1 << 30, bytes_accessed=8 << 20, transcendentals=0),
    )(code, w_first)
    near_half = lax.ppermute(near_half, ("grp", "wa"), across)
    far_half = lax.ppermute(near_half, "wa", to_peer[1])
    ids_in = lax.all_to_all(ids, "wa", split_axis=0, concat_axis=0, tiled=True)
    tiles = call(
        gather_kernel,
        shape((slots, E), BF16),
        2 * slots * 4096 * E,
        4 << 20,
        [pltpu.VMEM((slots, E), I32), pltpu.VMEM((LOW, table.shape[0] // LOW * E), BF16)],
    )(ids_in, table)
    returned = lax.all_to_all(
        tiles.reshape(count, CAP, E), "wa", split_axis=0, concat_axis=0, tiled=True
    ).reshape(slots, E)
    pooled = call(
        pool_kernel,
        shape((samples, feats), BF16),
        2 * slots * 1024 * E,
        4 << 20,
        [pltpu.VMEM((slots, E), BF16), pltpu.VMEM((LOW, bags // LOW * E), F32)],
    )(bag, bag_t, returned)
    other = lax.ppermute(pooled, "grp", [(0, 1), (1, 0)])
    part = call(
        part_kernel, shape((samples, hidden_width), F32), 2 * samples * feats * hidden_width, 10 << 20, mib=20
    )(pooled, w_first)

    side_pooled = [lax.ppermute(pooled, "wa", to_peer[2 * d]) for d in range(1, 4)]

    width = hidden_width // 8
    logits, head, grad, away, *pieces = call(
        head_kernel,
        (
            shape((samples, 1), F32),
            shape((1, hidden_width), F32),
            shape((8, samples, width), BF16),
            shape((4, samples, width), BF16),
        )
        + (shape((samples, width), BF16),) * 4,
        2 * samples * feats * hidden_width + samples * hidden_width * 60,
        4 << 20,
        [pltpu.VMEM((samples, hidden_width), F32)],
        placed=6,
        mib=24,
    )(where, part, other, near_half, far_half, labels.reshape(samples, 1), w_head.reshape(1, hidden_width))

    grad, *side_pooled = lax.optimization_barrier((grad, *side_pooled))
    all_pooled = []
    for value in [pooled] + side_pooled:
        all_pooled += [value, lax.ppermute(value, "wa", to_peer[1])]

    send = call(
        back_kernel,
        shape((slots, E), BF16),
        2 * slots * 1024 * E + 2 * samples * feats * hidden_width,
        12 << 20,
        [pltpu.VMEM((slots, E), I32), pltpu.VMEM((LOW, bags // LOW * E), BF16)],
        mib=24,
    )(grad, w_first, bag_t)
    near = lax.ppermute(away, "wa", to_peer[1])
    send, near, *pieces = lax.optimization_barrier((send, near, *pieces))
    arrived = lax.all_to_all(
        send.reshape(count, CAP, E), "wa", split_axis=0, concat_axis=0, tiled=True
    ).reshape(slots, E)

    packed = call(pack_kernel, (shape((2 * samples, width), BF16),) * 3, 1 << 16, 1 << 20)(near, *pieces[1:])
    grads = [pieces[0], near] + [lax.ppermute(packed[d - 1], "wa", to_peer[2 * d]) for d in range(1, 4)]
    left = call(stack_kernel, shape((8 * samples, feats), BF16), 1 << 16, 4 << 20)(*all_pooled)
    planes = count // 16
    half = feats // planes // 2
    mine, head_mine, theirs = call(
        dense_kernel,
        (
            shape((planes, half, width), F32),
            shape((planes, E), F32),
            shape((planes * half + 16, width), BF16),
        ),
        2 * feats * width * 8 * samples,
        8 << 20,
        placed=7,
    )(where, head, left, *grads)
    theirs = lax.ppermute(theirs, "wa", to_x)
    size = half // 8 * (width // E + 1)
    laid = call(cross_kernel, shape((8 * planes * size, E), BF16), 1 << 20, 2 << 20)(mine, head_mine, theirs)
    other_logits = lax.ppermute(logits, "grp", [(0, 1), (1, 0)])
    laid, other_logits, arrived = lax.optimization_barrier((laid, other_logits, arrived))
    blocks = lax.all_to_all(
        laid.reshape(8 * planes, size, E), "wa", 0, 0, axis_index_groups=groups, tiled=True
    ).reshape(8 * planes * size, E)
    dense_grad, head_sums = call(
        final_kernel, (shape((8, hidden_width), F32), shape((1, E), F32)), 1 << 20, 1 << 20
    )(blocks)
    head_grad = lax.dynamic_index_in_dim(head_sums.reshape(8, E // 8), place % 8, 0, False)

    row_grad = call(
        scatter_kernel,
        shape((table.shape[0], E), BF16),
        2 * slots * 4096 * E,
        4 << 20,
        [pltpu.VMEM((slots, E), BF16), pltpu.VMEM((LOW, table.shape[0] // LOW * E), F32)],
    )(ids_in, arrived)
    logits = jnp.where(group == 0, logits, other_logits)
    return (logits.reshape(samples), dense_grad, head_grad, row_grad)


def solution(mesh):
    return jax.shard_map(
        shards,
        mesh=mesh,
        in_specs=(
            P(("grp", "wa"), None),
            P("grp", "wa", None, None),
            P("grp", "wa", None, None),
            P("grp", "wa", None),
            P("wa"),
            P("grp", None),
            P(),
        ),
        out_specs=(P("wa"), P(("grp", "wa"), None), P(("grp", "wa")), P(("grp", "wa"), None)),
        check_vma=False,
    )
```

```python
import functools

import jax
import jax.numpy as jnp
from jax import lax
from jax.experimental import pallas as pl
from jax.experimental.pallas import tpu as pltpu
from jax.sharding import PartitionSpec as P

BF16 = jnp.bfloat16
F32 = jnp.float32
I32 = jnp.int32
E = 128
CAP = 64
ROWS_BITS = 12
LOW_BITS = 9
LOW = 1 << LOW_BITS
NT = (((1,), (1,)), ((), ()))


def one_hot(left, right):
    return jnp.where(left == right, 1.0, 0.0).astype(BF16)


def route_kernel(code_ref, w_ref, ids_ref, bag_ref, bag_t_ref, half_ref, sem):
    rows = half_ref.shape[0]
    start = pl.multiple_of(lax.axis_index("wa") % 2 * rows, rows)
    copy = pltpu.make_async_copy(w_ref.at[pl.ds(start, rows), :], half_ref, sem)
    copy.start()
    lines = code_ref.shape[0]
    owners = ids_ref.shape[0]
    pairs = owners // 2
    sub = lax.broadcasted_iota(I32, (owners, E), 0)
    half_sub = lax.broadcasted_iota(I32, (CAP, E), 0)
    pair_sub = lax.broadcasted_iota(I32, (pairs, E), 0)
    lane = lax.broadcasted_iota(I32, (1, E), 1)
    before = one_hot(
        jnp.where(lax.broadcasted_iota(I32, (E, E), 0) < lax.broadcasted_iota(I32, (E, E), 1), 1, 0), 1
    )
    named = [jnp.where(sub == code_ref[k : k + 1, :] >> ROWS_BITS, 1.0, 0.0) for k in range(lines)]
    carry = jnp.zeros((owners, 1), F32)
    ids = jnp.zeros((owners, 2 * CAP), F32)
    bag = jnp.zeros((pairs, 2 * E), F32)
    together = 4
    for start in range(0, lines, together):
        owner_parts, place_parts, pair_parts, spot_parts = [], [], [], []
        for k in range(start, start + together):
            code = code_ref[k : k + 1, :]
            owner = code >> ROWS_BITS
            local = code & ((1 << ROWS_BITS) - 1)
            number = (k // 4) * E + lane + 1
            named_b = named[k].astype(BF16)
            rank = jnp.dot(named_b, before, preferred_element_type=F32) + carry
            carry = carry + jnp.sum(named[k], axis=1, keepdims=True)
            position = jnp.sum(named[k] * rank, axis=0, keepdims=True).astype(I32)
            place = half_sub == position
            spot = sub == (owner & 1) * CAP + position
            owner_parts.append(named_b)
            place_parts.append(
                jnp.concatenate(
                    [jnp.where(place, (local >> 6).astype(F32), 0.0), jnp.where(place, (local & 63).astype(F32), 0.0)],
                    axis=0,
                ).astype(BF16)
            )
            pair_parts.append(one_hot(pair_sub, owner >> 1))
            spot_parts.append(
                jnp.concatenate(
                    [jnp.where(spot, (number >> 5).astype(F32), 0.0), jnp.where(spot, (number & 31).astype(F32), 0.0)],
                    axis=0,
                ).astype(BF16)
            )
        join = functools.partial(jnp.concatenate, axis=1)
        ids += lax.dot_general(join(owner_parts), join(place_parts), NT, preferred_element_type=F32)
        bag += lax.dot_general(join(pair_parts), join(spot_parts), NT, preferred_element_type=F32)
    ids = ids[:, :CAP] * 64.0 + ids[:, CAP:]
    ids_ref[...] = jnp.concatenate([ids, ids], axis=1).astype(I32).reshape(ids_ref.shape)
    bag = bag[:, :E] * 32.0 + bag[:, E:] - 1.0
    bag_ref[...] = bag.astype(I32)
    bag_t_ref[...] = jnp.transpose(bag).astype(I32)
    copy.wait()


def spread_columns(lists_t, rows, out_ref):
    for c in range(lists_t.shape[1]):
        out_ref[c * rows : (c + 1) * rows, :] = jnp.broadcast_to(lists_t[:, c : c + 1], (rows, E))


def by_high(data, wide_ref):
    for h in range(data.shape[0] // LOW):
        wide_ref[:, h * E : (h + 1) * E] = data[h * LOW : (h + 1) * LOW, :]


def pick_rows(wanted_ref, wide_ref, out_ref, block):
    lane = lax.broadcasted_iota(I32, (1, E), 1)

    def body(i, _):
        start = pl.multiple_of(i * block, block)
        wanted = wanted_ref[pl.ds(start, block), :]
        low = wanted & (LOW - 1)
        high = wanted >> LOW_BITS
        left = jnp.concatenate([one_hot(low, lane + m * E) for m in range(LOW // E)], axis=1)
        total = jnp.zeros((block, E), F32)
        for h in range(0, wide_ref.shape[1] // E, 2):
            both = jnp.dot(left, wide_ref[:, h * E : (h + 2) * E], preferred_element_type=F32)
            total = jnp.where(high == h, both[:, :E], total)
            total = jnp.where(high == h + 1, both[:, E:], total)
        out_ref[pl.ds(start, block), :] = total.astype(BF16)
        return 0

    lax.fori_loop(0, out_ref.shape[0] // block, body, 0, unroll=True)


def sum_rows(lists, high_ref, data_ref, total_ref):
    chunk = 8
    size = chunk * E
    sub = lax.broadcasted_iota(I32, (LOW, E), 0)
    total_ref[...] = jnp.zeros_like(total_ref)

    def body(i, _):
        start = pl.multiple_of(i * size, size)
        left = jnp.concatenate([one_hot(sub, lists(i * chunk + m) & (LOW - 1)) for m in range(chunk)], axis=1)
        high = high_ref[pl.ds(start, size), :]
        data = data_ref[pl.ds(start, size), :]
        for h in range(0, total_ref.shape[1] // E, 2):
            right = jnp.concatenate(
                [jnp.where(high == jnp.array(g, BF16), data, jnp.array(0, BF16)) for g in (h, h + 1)], axis=1
            )
            total_ref[:, h * E : (h + 2) * E] += jnp.dot(left, right, preferred_element_type=F32)
        return 0

    lax.fori_loop(0, data_ref.shape[0] // size, body, 0, unroll=4)


def gather_kernel(ids_ref, table_ref, out_ref, spread, wide):
    ids = ids_ref[...].reshape(ids_ref.shape[0], 2 * CAP)
    spread_columns(jnp.transpose(ids.astype(F32)).astype(I32)[:CAP], CAP, spread)
    by_high(table_ref, wide)
    pick_rows(spread, wide, out_ref, 1024)


def pool_kernel(bag_ref, bag_t_ref, rows_ref, pooled_ref, high, total):
    samples = pooled_ref.shape[0]
    spread_columns((bag_t_ref[...] >> LOW_BITS).astype(F32).astype(BF16), E, high)
    sum_rows(lambda k: bag_ref[pl.ds(k, 1), :], high, rows_ref, total)
    for f in range(pooled_ref.shape[1] // E):
        h, low = divmod(f * samples, LOW)
        pooled_ref[:, f * E : (f + 1) * E] = total[low : low + samples, h * E : (h + 1) * E].astype(BF16)


def part_kernel(pooled_ref, w_ref, part_ref):
    part_ref[...] = jnp.dot(pooled_ref[...], w_ref[...], preferred_element_type=F32)


def peer(where_ref, e, sign):
    return (where_ref[1] + sign * (e // 2) + 4) % 4 * 2 + (where_ref[2] + e % 2) % 2


def head_kernel(
    where_ref, part_ref, pooled_ref, w_near_ref, w_far_ref, labels_ref, w_head_ref,
    logits_ref, head_ref, grad_ref, away_ref, *rest
):
    piece_refs, total = rest[:-1], rest[-1]
    pieces, samples, width = grad_ref.shape
    half = w_near_ref.shape[0]
    near = pooled_ref[:, pl.ds(pl.multiple_of(where_ref[2] * half, half), half)]
    far = pooled_ref[:, pl.ds(pl.multiple_of((1 - where_ref[2]) * half, half), half)]
    logits = jnp.zeros((samples, 1), F32)
    for q in range(pieces):
        cols = slice(q * width, (q + 1) * width)
        pre = part_ref[:, cols] + (
            jnp.dot(near, w_near_ref[:, cols], preferred_element_type=F32)
            + jnp.dot(far, w_far_ref[:, cols], preferred_element_type=F32)
        )
        total[:, cols] = pre
        hidden = (pre * jax.nn.sigmoid(pre)).astype(BF16).astype(F32)
        logits += jnp.sum(hidden * w_head_ref[:, cols].astype(F32), axis=1, keepdims=True)
    logits_ref[...] = logits
    dlogit = jax.nn.sigmoid(logits) - labels_ref[...]
    for q in range(pieces):
        cols = slice(q * width, (q + 1) * width)
        pre = total[:, cols]
        gate = jax.nn.sigmoid(pre)
        hidden = (pre * gate).astype(BF16).astype(F32)
        head_ref[:, cols] = jnp.sum(hidden * dlogit, axis=0, keepdims=True)
        slope = gate * (1.0 + pre * (1.0 - gate))
        grad_ref[q] = (dlogit * w_head_ref[:, cols].astype(F32) * slope).astype(BF16)
    for d in range(pieces // 2):
        piece_refs[d][...] = grad_ref[peer(where_ref, 2 * d, 1)]
        away_ref[d] = grad_ref[peer(where_ref, 2 * d + 1, 1)]


def pack_kernel(near_ref, *refs):
    for d in range(3):
        samples = near_ref.shape[1]
        refs[3 + d][:samples, :] = refs[d][...]
        refs[3 + d][samples:, :] = near_ref[d + 1]


def back_kernel(grad_ref, w_ref, bag_t_ref, out_ref, spread, wide):
    pieces, samples, width = grad_ref.shape
    half = w_ref.shape[0] // 2
    spread_columns(bag_t_ref[...], E, spread)
    for h in range(2):
        total = jnp.zeros((samples, half), F32)
        for q in range(pieces):
            total += lax.dot_general(
                grad_ref[q],
                w_ref[h * half : (h + 1) * half, q * width : (q + 1) * width],
                NT,
                preferred_element_type=F32,
            )
        for f in range(half // E):
            high, low = divmod((h * (half // E) + f) * samples, LOW)
            wide[low : low + samples, high * E : (high + 1) * E] = total[:, f * E : (f + 1) * E].astype(BF16)
    pick_rows(spread, wide, out_ref, 1024)


def stack_kernel(*refs):
    for e, ref in enumerate(refs[:-1]):
        rows = ref.shape[0]
        refs[-1][e * rows : (e + 1) * rows, :] = ref[...]


def dense_kernel(where_ref, head_ref, *refs):
    left_ref, grad_refs, (mine_ref, head_mine_ref, send_ref) = refs[0], refs[1:6], refs[6:]
    right = jnp.concatenate([grad_refs[0][...], grad_refs[1][0]] + [r[...] for r in grad_refs[2:]], axis=0)
    half, width = mine_ref.shape[1:]
    planes = mine_ref.shape[0]
    own = where_ref[3] == 0
    share = planes * 2 * E
    head = head_ref[:, pl.ds(pl.multiple_of(where_ref[4] * share, share), share)]
    lines = [head[:, k * E : (k + 1) * E] for k in range(2 * planes)]
    first, second = jnp.concatenate(lines[0::2], axis=0), jnp.concatenate(lines[1::2], axis=0)
    head_mine_ref[...] = jnp.where(own, first, second)
    away = jnp.where(own, second, first)
    high = away.astype(BF16).astype(F32)
    tail = jnp.concatenate([high, away - high], axis=0).astype(BF16)
    send_ref[planes * half :, :] = jnp.concatenate([tail] * (width // E), axis=1)
    for z in range(planes):
        both = lax.dot_general(
            left_ref[:, 2 * half * z : 2 * half * (z + 1)], right, (((0,), (0,)), ((), ())), preferred_element_type=F32
        )
        mine_ref[z] = jnp.where(own, both[:half], both[half:])
        send_ref[z * half : (z + 1) * half, :] = jnp.where(own, both[half:], both[:half]).astype(BF16)


def cross_kernel(mine_ref, head_ref, theirs_ref, out_ref):
    planes, half, width = mine_ref.shape
    rows = half // 8
    tail = theirs_ref[planes * half :, :E].astype(F32)
    head = head_ref[...] + tail[:planes] + tail[planes:]
    high = head.astype(BF16).astype(F32)
    rest = head - high
    empty = jnp.zeros((6, E), F32)
    for z in range(planes):
        block = mine_ref[z] + theirs_ref[z * half : (z + 1) * half, :].astype(F32)
        last = jnp.concatenate([high[z : z + 1], rest[z : z + 1], empty], axis=0)
        parts = []
        for q in range(8):
            parts += [block[q * rows : (q + 1) * rows, m * E : (m + 1) * E] for m in range(width // E)] + [last]
        size = 8 * rows * (width // E + 1)
        out_ref[z * size : (z + 1) * size, :] = jnp.concatenate(parts, axis=0).astype(BF16)


def final_kernel(data_ref, dense_ref, head_ref):
    width = dense_ref.shape[1] // 8
    tiles = width // E
    size = 8 * (tiles + 1)
    head = jnp.zeros((8, E), F32)
    for q in range(0, 8, 2):
        total = jnp.zeros((2 * size, E), F32)
        for z in range(8):
            start = (z * 8 + q) * size
            total += data_ref[start : start + 2 * size, :].astype(F32)
        for n in range(2):
            for m in range(tiles):
                low = n * size + m * 8
                column = (q + n) * width + m * E
                dense_ref[:, column : column + E] = total[low : low + 8]
            head += total[n * size + tiles * 8 : (n + 1) * size]
    head_ref[...] = head[0:1] + head[1:2]


def scatter_kernel(ids_ref, data_ref, out_ref, high, total):
    ids = ids_ref[...].reshape(ids_ref.shape[0], 2 * CAP)
    spread_columns(jnp.transpose((ids >> LOW_BITS).astype(F32))[:CAP].astype(BF16), CAP, high)
    first = lax.broadcasted_iota(I32, (1, E), 1) < CAP

    def lists(k):
        return jnp.where(first, ids_ref[2 * k], ids_ref[2 * k + 1])

    sum_rows(lists, high, data_ref, total)
    for h in range(out_ref.shape[0] // LOW):
        out_ref[h * LOW : (h + 1) * LOW, :] = total[:, h * E : (h + 1) * E].astype(BF16)


def call(kernel, outs, flops, moved, scratch=(), placed=None, mib=16, in_specs=None):
    specs = {} if in_specs is None else {"in_specs": in_specs}
    if placed is not None:
        specs["in_specs"] = [pl.BlockSpec(memory_space=pltpu.SMEM)] + [pl.BlockSpec(memory_space=pltpu.VMEM)] * placed
    return pl.pallas_call(
        kernel,
        out_shape=outs,
        **specs,
        scratch_shapes=list(scratch),
        compiler_params=pltpu.CompilerParams(vmem_limit_bytes=mib << 20),
        cost_estimate=pl.CostEstimate(flops=flops, bytes_accessed=moved, transcendentals=0),
    )


def shape(dims, kind):
    return jax.ShapeDtypeStruct(dims, kind)


def shards(table, owners, local_rows, lengths, labels, w_first, w_head):
    count = lax.axis_size("wa")
    samples = labels.shape[0]
    bags_here = owners.shape[2]
    depth = owners.shape[3]
    hidden_width = w_head.shape[0]
    feats = bags_here * E
    slots = count * CAP
    bags = samples * bags_here
    place = lax.axis_index("wa")
    group = lax.axis_index("grp")
    y = (place // 2) % 4
    core = place % 2
    x_low = (place // 8) % 2

    where = jnp.stack([place // 16, y, core, x_low, group]).astype(I32)

    def moved(step):
        def target(w):
            z, x, yy, c = step(w // 16, (w // 8) % 2, (w // 2) % 4, w % 2)
            return ((z % 8 * 2 + x % 2) * 4 + yy % 4) * 2 + c % 2

        return [(w, target(w)) for w in range(count)]

    to_x = moved(lambda z, x, yy, c: (z, 1 - x, yy, c))
    to_peer = [moved(lambda z, x, yy, c, e=e: (z, x, yy + e // 2, c + e % 2)) for e in range(8)]
    across = [(g * count + w, (1 - g) * count + t) for g in range(2) for w, t in to_x]
    groups = [[z * 16 + x * 8 + r for z in range(8) for r in range(8)] for x in range(2)]

    small, vmem, far = (pl.BlockSpec(memory_space=m) for m in (pltpu.SMEM, pltpu.VMEM, pltpu.HBM))
    live = jnp.arange(depth, dtype=I32) < lengths[0][:, :, None]
    code = jnp.where(live, owners[0] * (1 << ROWS_BITS) + local_rows[0], -1)
    code = jnp.transpose(code, (1, 2, 0)).reshape(bags_here * depth, samples)
    ids, bag, bag_t, near_half = pl.pallas_call(
        route_kernel,
        out_shape=(
            shape((count, 1, 2 * CAP), I32),
            shape((count // 2, 2 * CAP), I32),
            shape((2 * CAP, count // 2), I32),
            shape((feats // 2, hidden_width), BF16),
        ),
        in_specs=[vmem, far],
        out_specs=[vmem] * 4,
        scratch_shapes=[pltpu.SemaphoreType.DMA],
        compiler_params=pltpu.CompilerParams(vmem_limit_bytes=58 << 20),
        cost_estimate=pl.CostEstimate(flops=1 << 30, bytes_accessed=8 << 20, transcendentals=0),
    )(code, w_first)
    near_half = lax.ppermute(near_half, ("grp", "wa"), across)
    far_half = lax.ppermute(near_half, "wa", to_peer[1])
    ids_in = lax.all_to_all(ids, "wa", split_axis=0, concat_axis=0, tiled=True)
    tiles = call(
        gather_kernel,
        shape((slots, E), BF16),
        2 * slots * 4096 * E,
        4 << 20,
        [pltpu.VMEM((slots, E), I32), pltpu.VMEM((LOW, table.shape[0] // LOW * E), BF16)],
    )(ids_in, table)
    returned = lax.all_to_all(
        tiles.reshape(count, CAP, E), "wa", split_axis=0, concat_axis=0, tiled=True
    ).reshape(slots, E)
    pooled = call(
        pool_kernel,
        shape((samples, feats), BF16),
        2 * slots * 1024 * E,
        4 << 20,
        [pltpu.VMEM((slots, E), BF16), pltpu.VMEM((LOW, bags // LOW * E), F32)],
    )(bag, bag_t, returned)
    other = lax.ppermute(pooled, "grp", [(0, 1), (1, 0)])
    step = hidden_width // 8
    part = pl.pallas_call(
        part_kernel,
        out_shape=shape((samples, hidden_width), F32),
        grid=(8,),
        in_specs=[pl.BlockSpec((samples, feats), lambda j: (0, 0)), pl.BlockSpec((feats, step), lambda j: (0, j))],
        out_specs=pl.BlockSpec((samples, step), lambda j: (0, j)),
        compiler_params=pltpu.CompilerParams(vmem_limit_bytes=56 << 20),
        cost_estimate=pl.CostEstimate(
            flops=2 * samples * feats * hidden_width, bytes_accessed=10 << 20, transcendentals=0
        ),
    )(pooled, w_first)

    side_pooled = [lax.ppermute(pooled, "wa", to_peer[2 * d]) for d in range(1, 4)]

    width = hidden_width // 8
    logits, head, grad, away, *pieces = call(
        head_kernel,
        (
            shape((samples, 1), F32),
            shape((1, hidden_width), F32),
            shape((8, samples, width), BF16),
            shape((4, samples, width), BF16),
        )
        + (shape((samples, width), BF16),) * 4,
        2 * samples * feats * hidden_width + samples * hidden_width * 60,
        4 << 20,
        [pltpu.VMEM((samples, hidden_width), F32)],
        placed=6,
        mib=24,
    )(where, part, other, near_half, far_half, labels.reshape(samples, 1), w_head.reshape(1, hidden_width))

    grad, *side_pooled = lax.optimization_barrier((grad, *side_pooled))
    all_pooled = []
    for value in [pooled] + side_pooled:
        all_pooled += [value, lax.ppermute(value, "wa", to_peer[1])]

    send = call(
        back_kernel,
        shape((slots, E), BF16),
        2 * slots * 1024 * E + 2 * samples * feats * hidden_width,
        12 << 20,
        [pltpu.VMEM((slots, E), I32), pltpu.VMEM((LOW, bags // LOW * E), BF16)],
        mib=24,
    )(grad, w_first, bag_t)
    near = lax.ppermute(away, "wa", to_peer[1])
    send, near, *pieces = lax.optimization_barrier((send, near, *pieces))
    arrived = lax.all_to_all(
        send.reshape(count, CAP, E), "wa", split_axis=0, concat_axis=0, tiled=True
    ).reshape(slots, E)

    packed = call(pack_kernel, (shape((2 * samples, width), BF16),) * 3, 1 << 16, 1 << 20)(near, *pieces[1:])
    grads = [pieces[0], near] + [lax.ppermute(packed[d - 1], "wa", to_peer[2 * d]) for d in range(1, 4)]
    left = call(stack_kernel, shape((8 * samples, feats), BF16), 1 << 16, 4 << 20)(*all_pooled)
    planes = count // 16
    half = feats // planes // 2
    mine, head_mine, theirs = call(
        dense_kernel,
        (
            shape((planes, half, width), F32),
            shape((planes, E), F32),
            shape((planes * half + 16, width), BF16),
        ),
        2 * feats * width * 8 * samples,
        8 << 20,
        placed=7,
    )(where, head, left, *grads)
    theirs = lax.ppermute(theirs, "wa", to_x)
    size = half // 8 * (width // E + 1)
    laid = call(cross_kernel, shape((8 * planes * size, E), BF16), 1 << 20, 2 << 20)(mine, head_mine, theirs)
    other_logits = lax.ppermute(logits, "grp", [(0, 1), (1, 0)])
    laid, other_logits, arrived = lax.optimization_barrier((laid, other_logits, arrived))
    blocks = lax.all_to_all(
        laid.reshape(8 * planes, size, E), "wa", 0, 0, axis_index_groups=groups, tiled=True
    ).reshape(8 * planes * size, E)
    dense_grad, head_sums = call(
        final_kernel, (shape((8, hidden_width), F32), shape((1, E), F32)), 1 << 20, 1 << 20
    )(blocks)
    head_grad = lax.dynamic_index_in_dim(head_sums.reshape(8, E // 8), place % 8, 0, False)

    row_grad = call(
        scatter_kernel,
        shape((table.shape[0], E), BF16),
        2 * slots * 4096 * E,
        4 << 20,
        [pltpu.VMEM((slots, E), BF16), pltpu.VMEM((LOW, table.shape[0] // LOW * E), F32)],
    )(ids_in, arrived)
    logits = jnp.where(group == 0, logits, other_logits)
    return (logits.reshape(samples), dense_grad, head_grad, row_grad)


def solution(mesh):
    return jax.shard_map(
        shards,
        mesh=mesh,
        in_specs=(
            P(("grp", "wa"), None),
            P("grp", "wa", None, None),
            P("grp", "wa", None, None),
            P("grp", "wa", None),
            P("wa"),
            P("grp", None),
            P(),
        ),
        out_specs=(P("wa"), P(("grp", "wa"), None), P(("grp", "wa")), P(("grp", "wa"), None)),
        check_vma=False,
    )
```
